256 devices in a mesh: rep: 8 (over y, core), shard: 32 (over z, x).
Axes of the slice: x: 4, y: 4, z: 8, core: 2. Of those that a mesh axis runs over, the one named last changes fastest.
Arguments:
- gu_slow: float32 [2, 256, 29568], P(None, 'shard'), may hold values from -6 to 6
- gu_fast: bfloat16 [8, 2, 256, 29568], P('rep', None, 'shard'), may hold values from -6 to 6
- gu_error: bfloat16 [8, 2, 256, 29568], P('rep', None, 'shard'), may hold values from -6 to 6
- gu_moment: float32 [2, 256, 29568], P(None, 'shard'), may hold values from -6 to 6
- gu_basis: bfloat16 [29568, 128], P('shard'), may hold values from -0.03125 to 0.03125
- dn_slow: float32 [256, 8192], P('shard'), may hold values from -6 to 6
- dn_fast: bfloat16 [8, 256, 8192], P('rep', 'shard'), may hold values from -6 to 6
- dn_error: bfloat16 [8, 256, 8192], P('rep', 'shard'), may hold values from -6 to 6
- dn_moment: float32 [256, 8192], P('shard'), may hold values from -6 to 6
- dn_basis: bfloat16 [8192, 64], P('shard'), may hold values from -0.0625 to 0.0625
Outputs:
- gu_slow_next: float32 [2, 256, 29568], P(None, 'shard')
- gu_error_next: bfloat16 [8, 2, 256, 29568], P('rep', None, 'shard')
- gu_moment_next: float32 [2, 256, 29568], P(None, 'shard')
- gu_basis_next: bfloat16 [29568, 128], P('shard')
- dn_slow_next: float32 [256, 8192], P('shard')
- dn_error_next: bfloat16 [8, 256, 8192], P('rep', 'shard')
- dn_moment_next: float32 [256, 8192], P('shard')
- dn_basis_next: bfloat16 [8192, 64], P('shard')
The draws below stay inside these ranges and needn't reach their ends.
All inputs are finite; a program needn't handle non-finite values.
Results may differ from the reference program's by a relative error of at most 0.014.
Values may be sent and summed in bfloat16 or wider, within the bound.
No kernel may reach another device: no remote copies, remote signals or barrier semaphores. Data moves between devices by JAX's collectives and lax.ppermute only.
A program may use at most 128 MiB of HBM per device.

```python
import jax
import jax.numpy as jnp
from jax import lax

D = 8192
FF = 29568
RANK = 64
ROWS = 256
REPS = 8


def block_scale(stream_key, extent, pieces, low, largest):
    loudness, own = 1.0, jax.random.fold_in(stream_key, 6)
    for position, shards_of in pieces:
        steps = jnp.exp(jax.random.uniform(jax.random.fold_in(own, position), (shards_of,), jnp.float32, low / len(pieces), largest / len(pieces)))
        loudness = loudness * jnp.repeat(steps, extent[position] // shards_of).reshape([-1 if axis == position else 1 for axis in range(len(extent))])
    return loudness


def normal_values(own_key, dims, width, limit, cuts=(), kind=jnp.bfloat16):
    values = jax.random.normal(own_key, dims, jnp.float32) * width
    if len(cuts) > 0:
        values = block_scale(own_key, dims, cuts, -0.22, 0.18) * values
    return jnp.clip(values, min=-limit, max=limit).astype(kind)


def setup_inputs(seed: int = 0) -> dict:
    key_list = jax.random.split(jax.random.key(seed), 11)
    return {
        "gu_slow": normal_values(key_list[0], (2, ROWS, FF), 1.0, 6.0, ((1, 32),), jnp.float32),
        "gu_fast": normal_values(key_list[1], (REPS, 2, ROWS, FF), 1.0, 6.0, ((0, 8), (2, 32))),
        "gu_error": normal_values(key_list[2], (REPS, 2, ROWS, FF), 0.5, 6.0, ((0, 8), (2, 32))),
        "gu_moment": normal_values(key_list[3], (2, ROWS, FF), 0.5, 6.0, ((1, 32),), jnp.float32),
        "gu_basis": normal_values(key_list[4], (FF, 2 * RANK), FF ** -0.5, 0.03125, ((0, 32),)),
        "dn_slow": normal_values(key_list[5], (ROWS, D), 1.0, 6.0, ((0, 32),), jnp.float32),
        "dn_fast": normal_values(key_list[6], (REPS, ROWS, D), 1.0, 6.0, ((0, 8), (1, 32))),
        "dn_error": normal_values(key_list[7], (REPS, ROWS, D), 0.5, 6.0, ((0, 8), (1, 32))),
        "dn_moment": normal_values(key_list[8], (ROWS, D), 0.5, 6.0, ((0, 32),), jnp.float32),
        "dn_basis": normal_values(key_list[9], (D, RANK), D ** -0.5, 0.0625, ((0, 32),)),
    }


def orthonormal(p_mean, gram_matrix):
    lower = jnp.linalg.cholesky(gram_matrix)
    return lax.linalg.triangular_solve(lower, p_mean, left_side=False, lower=True, transpose_a=True)

def compress(slow, fast, error, moment, basis):
    matrices, local_rows, columns_total = slow.shape
    factor = basis.reshape(columns_total, matrices, RANK).astype(jnp.float32)
    p_acc = jnp.zeros((matrices, local_rows, RANK), jnp.float32)
    for replica in range(REPS):
        combined = slow - fast[replica].astype(jnp.float32) + error[replica].astype(jnp.float32)
        lowered = combined.astype(jnp.bfloat16).astype(jnp.float32)
        p_acc = p_acc + jnp.einsum('brn,nbk->brk', lowered, factor)
    p_mean = p_acc / REPS
    gram_matrix = jnp.einsum('brk,brl->bkl', p_mean, p_mean, precision=lax.Precision.HIGHEST)
    left_basis = orthonormal(p_mean, gram_matrix).astype(jnp.bfloat16).astype(jnp.float32)
    q_acc = jnp.zeros((columns_total, matrices, RANK), jnp.float32)
    for replica in range(REPS):
        combined = slow - fast[replica].astype(jnp.float32) + error[replica].astype(jnp.float32)
        lowered = combined.astype(jnp.bfloat16).astype(jnp.float32)
        q_acc = q_acc + jnp.einsum('brn,brk->nbk', lowered, left_basis)
    q_low = (q_acc / REPS).astype(jnp.bfloat16)
    recon = jnp.einsum('brk,nbk->brn', left_basis, q_low.astype(jnp.float32)).astype(jnp.bfloat16)
    recon = lax.optimization_barrier(recon).astype(jnp.float32)
    errors = []
    for replica in range(REPS):
        combined = slow - fast[replica].astype(jnp.float32) + error[replica].astype(jnp.float32)
        errors.append((combined - recon).astype(jnp.bfloat16))
    moment_next = 0.9 * moment + recon
    slow_next = slow - 0.7 * (recon + 0.9 * moment_next)
    return (slow_next, jnp.stack(errors), moment_next, q_low.reshape(columns_total, matrices * RANK))

def reference(gu_slow, gu_fast, gu_error, gu_moment, gu_basis, dn_slow, dn_fast, dn_error, dn_moment, dn_basis):
    gs, ge, gm, gb = compress(gu_slow, gu_fast, gu_error, gu_moment, gu_basis)
    ds, de, dm, db = compress(dn_slow[None], dn_fast[:, None], dn_error[:, None], dn_moment[None], dn_basis)
    return (gs, ge, gm, gb, ds[0], de[:, 0], dm[0], db)
```

```python
import functools

import jax
import jax.numpy as jnp
from jax import lax
from jax.experimental import pallas as pl
from jax.experimental.pallas import tpu as pltpu
from jax.sharding import Mesh
from jax.sharding import PartitionSpec as P

FF = 29568
D = 8192
SHARDS = 32
REPS = 8
GU_COLS = FF // SHARDS
DN_COLS = D // SHARDS
GU_SUB = 116
DN_SUB = DN_COLS // REPS
LANES = 128
FF_PAD = FF + LANES
D_PAD = D + LANES
RANK = 64
F32 = jnp.float32
BF16 = jnp.bfloat16
SHARD = ("z", "x")
VMEM = pl.BlockSpec(memory_space=pltpu.VMEM)
SMEM = pl.BlockSpec(memory_space=pltpu.SMEM)
ANY = pl.BlockSpec(memory_space=pl.ANY)
GROUPS = 4


def params(mib):
    return pltpu.CompilerParams(vmem_limit_bytes=mib * 2**20)


def up_to(value, unit):
    return -(-value // unit) * unit


def piece_bounds():
    per = SHARDS // GROUPS
    gu, dn = [0], [0]
    for g in range(GROUPS):
        gu.append(min(FF, up_to(GU_COLS * per * (g + 1) + 32, LANES)))
        dn.append(min(D, DN_COLS * per * (g + 1) + LANES))
    gu[-1], dn[-1] = FF, D
    return gu, dn


def lower_kernel(pos, gs, gf, ge, ds, df, de, own, oth, gsv, gfv, gev, dsv, dfv, dev, sems):
    y, core = pos[0], pos[1]
    gu_at, dn_at = piece_bounds()
    copies = []
    for g in range(GROUPS):
        a, n = gu_at[g], gu_at[g + 1] - gu_at[g]
        c, m = dn_at[g], dn_at[g + 1] - dn_at[g]
        row = []
        for i, (src, dst) in enumerate(((gs, gsv), (gf, gfv), (ge, gev))):
            at = (slice(None), slice(None), pl.ds(a, n))
            row.append(pltpu.make_async_copy(src.at[at], dst.at[at], sems.at[g, i]))
        for i, (src, dst) in enumerate(((ds, dsv), (df, dfv), (de, dev))):
            at = (slice(None), pl.ds(c, m))
            row.append(pltpu.make_async_copy(src.at[at], dst.at[at], sems.at[g, 3 + i]))
        for copy in row:
            copy.start()
        copies.append(row)
    for ref in (gsv, gfv, gev):
        ref[:, :, FF:] = jnp.zeros((2, 8, LANES), ref.dtype)
    for ref in (dsv, dfv, dev):
        ref[:, D:] = jnp.zeros((8, LANES), ref.dtype)
    first = core == 0
    per = SHARDS // GROUPS
    for shard in range(SHARDS):
        if shard % per == 0:
            for copy in copies[shard // per]:
                copy.wait()
        start = GU_COLS * shard
        base = start // LANES * LANES
        end = up_to(start + GU_SUB * 7 + LANES, LANES)
        at = (slice(None), slice(None), slice(base, end))
        gu = gsv[at] - gfv[at].astype(F32) + gev[at].astype(F32)
        dn_start = DN_COLS * shard
        at = (slice(None), slice(dn_start, dn_start + DN_COLS + LANES))
        dn = dsv[at] - dfv[at].astype(F32) + dev[at].astype(F32)
        for yy in range(4):
            slot = lax.rem(yy - y + 4, 4)
            parts = []
            for c in range(2):
                r = 2 * yy + c
                o = start - base + GU_SUB * r
                parts.append(
                    jnp.concatenate(
                        [
                            gu[0, :, o : o + LANES],
                            gu[1, :, o : o + LANES],
                            dn[:, DN_SUB * r : DN_SUB * r + LANES],
                        ],
                        axis=0,
                    )
                )
            own[slot, shard] = jnp.where(first, parts[0], parts[1]).astype(BF16)
            oth[slot, shard] = jnp.where(first, parts[1], parts[0]).astype(BF16)


def lower(pos, gs, gf, ge, ds, df, de):
    shape = jax.ShapeDtypeStruct((4, SHARDS, 24, LANES), BF16)
    return pl.pallas_call(
        lower_kernel,
        out_shape=(shape, shape),
        in_specs=[SMEM] + [ANY] * 6,
        out_specs=(VMEM, VMEM),
        scratch_shapes=[
            pltpu.VMEM((2, 8, FF_PAD), F32),
            pltpu.VMEM((2, 8, FF_PAD), BF16),
            pltpu.VMEM((2, 8, FF_PAD), BF16),
            pltpu.VMEM((8, D_PAD), F32),
            pltpu.VMEM((8, D_PAD), BF16),
            pltpu.VMEM((8, D_PAD), BF16),
            pltpu.SemaphoreType.DMA((GROUPS, 6)),
        ],
        compiler_params=params(32),
    )(pos, gs, gf, ge, ds, df, de)


def split_hi_lo(value):
    hi = value.astype(BF16).astype(F32)
    return jnp.concatenate([hi, value - hi], axis=-1).astype(BF16)


def p_part_kernel(lx, bz, out):
    acc_gu = jnp.zeros((96, LANES), F32)
    acc_dn = jnp.zeros((96, LANES), F32)
    for z in range(8):
        lhs = lx[:, z].astype(F32).reshape(96, LANES).astype(BF16)
        acc_gu = acc_gu + jnp.dot(lhs, bz[z, 0:128, :], preferred_element_type=F32)
        acc_dn = acc_dn + jnp.dot(lhs[:, 0:32], bz[z, 128:160, :], preferred_element_type=F32)
    acc_gu = acc_gu.reshape(4, 24, LANES)
    acc_dn = acc_dn.reshape(4, 24, LANES)
    part = jnp.concatenate(
        [acc_gu[:, 0:8, 0:RANK], acc_gu[:, 8:16, RANK:LANES], acc_dn[:, 16:24, 0:RANK]], axis=1
    )
    block = split_hi_lo(part)
    for rep in range(REPS):
        out[4 * rep : 4 * rep + 4] = block


def p_part(lx, bz):
    return pl.pallas_call(
        p_part_kernel,
        out_shape=jax.ShapeDtypeStruct((32, 24, LANES), BF16),
        in_specs=[VMEM, VMEM],
        out_specs=VMEM,
        compiler_params=params(16),
    )(lx, bz)


def p_sum_kernel(ps, lbar, out):
    total = jnp.sum(ps[...].astype(F32), axis=0)
    rows = split_hi_lo(total[:, 0:RANK] + total[:, RANK:LANES])
    out[:, 0:24, :] = lbar[...]
    out[:, 24:48, :] = jnp.broadcast_to(rows[None], (SHARDS, 24, LANES))


def p_sum(ps, lbar):
    return pl.pallas_call(
        p_sum_kernel,
        out_shape=jax.ShapeDtypeStruct((SHARDS, 48, LANES), BF16),
        in_specs=[VMEM, VMEM],
        out_specs=VMEM,
        compiler_params=params(16),
    )(ps, lbar)


def inverse_factors(grams):
    eye = (
        lax.broadcasted_iota(jnp.int32, (RANK, RANK), 0)
        == lax.broadcasted_iota(jnp.int32, (RANK, RANK), 1)
    ).astype(F32)
    blocks = []
    for gram in grams:
        work = jnp.concatenate([gram, eye], axis=1)
        blocks.append([work[8 * b : 8 * b + 8] for b in range(8)])
    sub = lax.broadcasted_iota(jnp.int32, (8, LANES), 0)
    rows = [[] for _ in grams]
    for k in range(RANK):
        b0, s = k // 8, k % 8
        for m, work in enumerate(blocks):
            row = jnp.broadcast_to(work[b0][s : s + 1], (8, LANES))
            cols = [jnp.broadcast_to(work[b][:, k : k + 1], (8, LANES)) for b in range(b0, 8)]
            pivot = jnp.broadcast_to(cols[0][s : s + 1], (8, LANES))
            rows[m].append((row * lax.rsqrt(pivot))[0:1])
            scaled = row / pivot
            for b in range(b0, 8):
                factor = cols[b - b0]
                if b == b0:
                    if s == 7:
                        continue
                    factor = jnp.where(sub > s, factor, 0.0)
                work[b] = work[b] - factor * scaled
    return [jnp.concatenate(r, axis=0)[:, RANK:LANES] for r in rows]


def exact_dot(a, b, dims):
    return lax.dot_general(
        a, b, (dims, ((), ())), precision=lax.Precision.HIGHEST, preferred_element_type=F32
    )


def factor_kernel(recv, a_out, q_out):
    block = recv[...].astype(F32)
    columns = [
        block[:, 8 * m : 8 * m + 8, :].reshape(256, LANES).astype(BF16) for m in range(3)
    ]
    left = block[:, 24:48, :]
    left = left[:, :, 0:RANK] + left[:, :, RANK:LANES]
    lefts = [left[:, 8 * m : 8 * m + 8, :].reshape(256, RANK) for m in range(3)]
    grams = [exact_dot(p, p, ((0,), (0,))) for p in lefts]
    inverses = inverse_factors(grams)
    qs, recons = [], []
    for p, inverse, column in zip(lefts, inverses, columns):
        h = exact_dot(p, inverse, ((1,), (1,))).astype(BF16)
        q = lax.dot_general(column, h, (((0,), (0,)), ((), ())), preferred_element_type=F32)
        q = (q * (1.0 / REPS)).astype(BF16)
        qs.append(q)
        recon = lax.dot_general(h, q, (((1,), (1,)), ((), ())), preferred_element_type=F32)
        recons.append(recon.reshape(SHARDS, 8, LANES))
    a_out[...] = jnp.concatenate(recons, axis=1).astype(BF16)
    q_out[0:128, :] = jnp.concatenate([qs[0].astype(F32), qs[1].astype(F32)], axis=1).astype(BF16)
    dn = qs[2].astype(F32)[0:DN_SUB]
    q_out[128:160, :] = jnp.concatenate([dn, jnp.zeros_like(dn)], axis=1).astype(BF16)


def factor(recv):
    return pl.pallas_call(
        factor_kernel,
        out_shape=(
            jax.ShapeDtypeStruct((SHARDS, 24, LANES), BF16),
            jax.ShapeDtypeStruct((160, LANES), BF16),
        ),
        in_specs=[VMEM],
        out_specs=(VMEM, VMEM),
        compiler_params=params(32),
    )(recv)


STEPS = 8
GU_TILE = 29 * LANES
DN_TILE = D // STEPS
PAYLOAD = SHARDS * 24 + 160


def finish_kernel(
    pos, b0, b1, b2, b3, b4, b5, b6, b7, gs, gf, ge, gm, ds, df, de, dm,
    gs_o, ge_o, gm_o, ds_o, de_o, dm_o, gb_o, db_o, stage, gu_full, dn_full, q_full, sems,
):
    step = pl.program_id(0)

    @pl.when(step == 0)
    def _():
        y, core = pos[0], pos[1]
        copies = []
        for i, ref in enumerate((b0, b1, b2, b3, b4, b5, b6, b7)):
            whose = lax.rem(y - i % 4 + 4, 4)
            side = core if i < 4 else 1 - core
            copies.append(
                pltpu.make_async_copy(ref, stage.at[2 * whose + side], sems.at[i])
            )
            copies[-1].start()
        for copy in copies:
            copy.wait()
        for shard in range(SHARDS):
            for r in range(REPS):
                block = stage[r, 24 * shard : 24 * shard + 24, :].astype(F32)
                at = GU_COLS * shard + GU_SUB * r
                gu_full[0, :, at : at + LANES] = block[0:8]
                gu_full[1, :, at : at + LANES] = block[8:16]
                at = DN_COLS * shard + DN_SUB * r
                dn_full[:, at : at + LANES] = block[16:24]
        for r in range(REPS):
            q_full[GU_SUB * r : GU_SUB * r + 128, :] = stage[r, 768:896, :].astype(F32)
        gb_o[...] = q_full[0:GU_COLS, :].astype(BF16)
        for r in range(REPS):
            db_o[DN_SUB * r : DN_SUB * r + DN_SUB, :] = stage[r, 896:928, :][:, 0:RANK]

    def outer(slow, fast, error, moment, recon):
        combined = slow - fast.astype(F32) + error.astype(F32)
        moment_next = 0.9 * moment + recon
        return (
            slow - 0.7 * (recon + 0.9 * moment_next),
            (combined - recon).astype(BF16),
            moment_next,
        )

    recon = gu_full[:, :, pl.ds(pl.multiple_of(step * GU_TILE, LANES), GU_TILE)]
    gs_o[...], e, gm_o[...] = outer(gs[...], gf[0], ge[0], gm[...], recon)
    ge_o[...] = e[None]
    recon = dn_full[:, pl.ds(pl.multiple_of(step * DN_TILE, LANES), DN_TILE)]
    ds_o[...], e, dm_o[...] = outer(ds[...], df[0], de[0], dm[...], recon)
    de_o[...] = e[None]


def finish(pos, blocks, gs, gf, ge, gm, ds, df, de, dm):
    gu = pl.BlockSpec((2, 8, GU_TILE), lambda i: (0, 0, i))
    gu1 = pl.BlockSpec((1, 2, 8, GU_TILE), lambda i: (0, 0, 0, i))
    dn = pl.BlockSpec((8, DN_TILE), lambda i: (0, i))
    dn1 = pl.BlockSpec((1, 8, DN_TILE), lambda i: (0, 0, i))

    def like(a):
        return jax.ShapeDtypeStruct(a.shape, a.dtype)

    return pl.pallas_call(
        finish_kernel,
        grid=(STEPS,),
        out_shape=(
            like(gs), like(ge), like(gm), like(ds), like(de), like(dm),
            jax.ShapeDtypeStruct((GU_COLS, LANES), BF16),
            jax.ShapeDtypeStruct((DN_COLS, RANK), BF16),
        ),
        in_specs=[SMEM] + [ANY] * 8 + [gu, gu1, gu1, gu, dn, dn1, dn1, dn],
        out_specs=(
            gu, gu1, gu, dn, dn1, dn,
            pl.BlockSpec((GU_COLS, LANES), lambda i: (0, 0)),
            pl.BlockSpec((DN_COLS, RANK), lambda i: (0, 0)),
        ),
        scratch_shapes=[
            pltpu.VMEM((REPS, PAYLOAD, LANES), BF16),
            pltpu.VMEM((2, 8, GU_TILE * STEPS), F32),
            pltpu.VMEM((8, D_PAD), F32),
            pltpu.VMEM((960, LANES), F32),
            pltpu.SemaphoreType.DMA((8,)),
        ],
        compiler_params=params(40),
    )(pos, *blocks, gs, gf, ge, gm, ds, df, de, dm)


def shift(value, axis, size, by):
    return lax.ppermute(value, axis, [(i, (i + by) % size) for i in range(size)])


def swap(value):
    return lax.ppermute(value, "core", [(0, 1), (1, 0)])


def exchange(value, axis):
    return lax.all_to_all(value, axis, 0, 0, tiled=False)


def on_device(
    gu_slow, gu_fast, gu_error, gu_moment, gu_basis, dn_slow, dn_fast, dn_error, dn_moment, dn_basis
):
    y, core = lax.axis_index("y"), lax.axis_index("core")
    rep = 2 * y + core
    pos = jnp.stack([y, core]).astype(jnp.int32)
    own, oth = lower(pos, gu_slow, gu_fast[0], gu_error[0], dn_slow, dn_fast[0], dn_error[0])
    came = swap(oth)
    pair = own.astype(F32) + came.astype(F32)
    sends = {by: pair[by].astype(BF16) for by in (2, 1, 3)}
    comes = {by: shift(sends[by], "y", 4, by) for by in (2, 1, 3)}

    gu_b = jnp.pad(gu_basis, ((0, 4), (0, 0)))
    gu_b = jnp.pad(lax.dynamic_slice(gu_b, (GU_SUB * rep, 0), (GU_SUB, LANES)), ((0, 12), (0, 0)))
    dn_b = lax.dynamic_slice(dn_basis, (DN_SUB * rep, 0), (DN_SUB, RANK))
    b_own = jnp.concatenate([gu_b, jnp.pad(dn_b, ((0, 0), (0, RANK)))], axis=0)
    b_z = exchange(jnp.broadcast_to(b_own[None], (8, 160, LANES)), "z")

    total = pair[0] + comes[1].astype(F32) + comes[2].astype(F32) + comes[3].astype(F32)
    lbar = total.astype(BF16)
    l_x = exchange(jnp.swapaxes(lbar.reshape(8, 4, 24, LANES), 0, 1), "x")
    parts = exchange(p_part(l_x, b_z), ("y", "core", "x"))
    recv = exchange(p_sum(parts, lbar), SHARD)
    a_blocks, q_block = factor(recv)
    a_rows = exchange(a_blocks, SHARD)
    payload = jnp.concatenate([a_rows.reshape(SHARDS * 24, LANES), q_block], axis=0)
    mine = {0: payload}
    for by in (2, 1, 3):
        mine[by] = shift(payload, "y", 4, by)
    blocks = [mine[by] for by in range(4)]
    blocks = blocks + [swap(b) for b in blocks]
    gs, ge, gm, ds, de, dm, gb, db = finish(
        pos, blocks, gu_slow, gu_fast, gu_error, gu_moment, dn_slow, dn_fast, dn_error, dn_moment
    )
    return gs, ge, gm, gb, ds, de, dm, db


def solution(mesh):
    fine = Mesh(mesh.devices.reshape(4, 2, 8, 4), ("y", "core", "z", "x"))
    rep = ("y", "core")
    weights, shared = P(None, SHARD, None), P(SHARD, None)
    replica = P(rep, None, SHARD, None)
    dn_replica = P(rep, SHARD, None)
    return jax.shard_map(
        on_device,
        mesh=fine,
        in_specs=(
            weights, replica, replica, weights, shared,
            shared, dn_replica, dn_replica, shared, shared,
        ),
        out_specs=(
            weights, replica, weights, shared,
            shared, dn_replica, shared, shared,
        ),
        check_vma=False,
    )
```

```python
import functools

import jax
import jax.numpy as jnp
from jax import lax
from jax.experimental import pallas as pl
from jax.experimental.pallas import tpu as pltpu
from jax.sharding import Mesh
from jax.sharding import PartitionSpec as P

FF = 29568
D = 8192
SHARDS = 32
REPS = 8
GU_COLS = FF // SHARDS
DN_COLS = D // SHARDS
LANES = 128
TILES = FF // LANES
RANK = 64
F32 = jnp.float32
BF16 = jnp.bfloat16
SHARD = ("z", "x")
VMEM = pl.BlockSpec(memory_space=pltpu.VMEM)
SMEM = pl.BlockSpec(memory_space=pltpu.SMEM)
ANY = pl.BlockSpec(memory_space=pl.ANY)
GROUPS = 4
PER = SHARDS // GROUPS


def params(mib):
    return pltpu.CompilerParams(vmem_limit_bytes=mib * 2**20)


def first_tile(shard):
    return TILES * shard // SHARDS


def offset(shard):
    return GU_COLS * shard - LANES * first_tile(shard)


def has_ninth(shard):
    return offset(shard) > 8 * LANES - GU_COLS


def lane_ids():
    return lax.broadcasted_iota(jnp.int32, (8, LANES), 1)


def group_bounds():
    bounds = [0]
    for g in range(GROUPS):
        bounds.append(min(TILES, first_tile(PER * (g + 1)) + 1) * LANES)
    return bounds


GU_ROWS = SHARDS * 16
DN_TILES = D // REPS // LANES
BLOCK = GU_ROWS + DN_TILES * 8


def lower_kernel(pos, gs, gf, ge, ds, df, de, own, oth, gsv, gfv, gev, dsv, dfv, dev, sems):
    y, core = pos[0], pos[1]
    bounds = group_bounds()
    copies = []
    for g in range(GROUPS):
        a, n = bounds[g], bounds[g + 1] - bounds[g]
        c, m = DN_COLS * PER * g, DN_COLS * PER
        row = []
        for i, (src, dst) in enumerate(((gs, gsv), (gf, gfv), (ge, gev))):
            at = (slice(None), slice(None), pl.ds(a, n))
            row.append(pltpu.make_async_copy(src.at[at], dst.at[at], sems.at[g, i]))
        for i, (src, dst) in enumerate(((ds, dsv), (df, dfv), (de, dev))):
            at = (slice(None), pl.ds(c, m))
            row.append(pltpu.make_async_copy(src.at[at], dst.at[at], sems.at[g, 3 + i]))
        for copy in row:
            copy.start()
        copies.append(row)
    first = core == 0
    lane = lane_ids()
    slots = [lax.rem(yy - y + 4, 4) for yy in range(4)]

    def gu_tile(tile):
        at = (slice(None), slice(None), pl.ds(tile * LANES, LANES))
        return gsv[at] - gfv[at].astype(F32) + gev[at].astype(F32)

    for shard in range(SHARDS):
        if shard % PER == 0:
            for copy in copies[shard // PER]:
                copy.wait()
        tiles = [gu_tile(first_tile(shard) + j) for j in range(8)]
        if has_ninth(shard):
            tiles[0] = jnp.where(lane[None] < 24, gu_tile(first_tile(shard) + 8), tiles[0])
        for yy in range(4):
            one, two = (tiles[2 * yy + c].reshape(16, LANES) for c in range(2))
            at = slice(16 * shard, 16 * shard + 16)
            own[slots[yy], at] = jnp.where(first, one, two).astype(BF16)
            oth[slots[yy], at] = jnp.where(first, two, one).astype(BF16)
    for half in range(DN_TILES // 2):
        parts = [[None, None] for _ in range(REPS)]
        for k in range(2):
            wide = pl.ds(4 * DN_COLS * (2 * half + k), 4 * DN_COLS)
            dn = dsv[:, wide] - dfv[:, wide].astype(F32) + dev[:, wide].astype(F32)
            for r in range(REPS):
                tile = None
                for a in range(4):
                    at = DN_COLS * a + LANES * (r // 4)
                    piece = dn[:, at : at + LANES]
                    if a != r % 4:
                        piece = pltpu.roll(piece, 32 * (a - r % 4) % LANES, 1)
                    tile = piece if a == 0 else jnp.where(lane < 32 * a, tile, piece)
                parts[r][k] = tile
        for yy in range(4):
            one, two = (jnp.concatenate(parts[2 * yy + c], axis=0) for c in range(2))
            at = slice(GU_ROWS + 16 * half, GU_ROWS + 16 * half + 16)
            own[slots[yy], at] = jnp.where(first, one, two).astype(BF16)
            oth[slots[yy], at] = jnp.where(first, two, one).astype(BF16)


def lower(pos, gs, gf, ge, ds, df, de):
    shape = jax.ShapeDtypeStruct((4, BLOCK, LANES), BF16)
    return pl.pallas_call(
        lower_kernel,
        out_shape=(shape, shape),
        in_specs=[SMEM] + [ANY] * 6,
        out_specs=(VMEM, VMEM),
        scratch_shapes=[
            pltpu.VMEM((2, 8, FF), F32),
            pltpu.VMEM((2, 8, FF), BF16),
            pltpu.VMEM((2, 8, FF), BF16),
            pltpu.VMEM((8, D), F32),
            pltpu.VMEM((8, D), BF16),
            pltpu.VMEM((8, D), BF16),
            pltpu.SemaphoreType.DMA((GROUPS, 6)),
        ],
        compiler_params=params(56),
    )(pos, gs, gf, ge, ds, df, de)


B_ROWS = LANES + 16


def basis_kernel(pos, gu, dn_t, out, rows, dn_rows):
    rep, shard = 2 * pos[0] + pos[1], pos[2]
    start = LANES - offset(shard)
    rows[0:LANES, :] = jnp.zeros((LANES, LANES), F32)
    rows[LANES : LANES + GU_COLS, :] = gu[...].astype(F32)
    rows[LANES + GU_COLS :, :] = jnp.zeros((rows.shape[0] - LANES - GU_COLS, LANES), F32)
    tile = rows[pl.ds(start + LANES * rep, LANES), :]
    ninth = rows[pl.ds(start + LANES * 8, LANES), :]
    tile = tile + jnp.where(rep == 0, ninth, 0.0)
    dn_rows[...] = dn_t[...].astype(F32).T
    dn = dn_rows[pl.ds(pl.multiple_of(32 * rep, 32), 32), :]
    dn = jnp.concatenate([dn[0:16], dn[16:32]], axis=1)
    block = jnp.concatenate([tile, dn], axis=0).astype(BF16)
    for s in range(SHARDS):
        out[s] = block


def basis_tiles(pos, gu, dn_t):
    return pl.pallas_call(
        basis_kernel,
        out_shape=jax.ShapeDtypeStruct((SHARDS, B_ROWS, LANES), BF16),
        in_specs=[SMEM, VMEM, VMEM],
        out_specs=VMEM,
        scratch_shapes=[pltpu.VMEM((1280, LANES), F32), pltpu.VMEM((DN_COLS, RANK), F32)],
        compiler_params=params(16),
    )(pos, gu, dn_t)


def y_sum_kernel(own, came, one, two, three, out):
    for at in range(0, BLOCK, 64):
        rows = slice(at, at + 64)
        total = own[0, rows].astype(F32) + came[0, rows].astype(F32)
        for ref in (one, two, three):
            total = total + ref[rows].astype(F32)
        out[rows] = total.astype(BF16)


def y_sum(own, came, comes):
    return pl.pallas_call(
        y_sum_kernel,
        out_shape=jax.ShapeDtypeStruct((BLOCK, LANES), BF16),
        in_specs=[VMEM] * 5,
        out_specs=VMEM,
        compiler_params=params(16),
    )(own, came, comes[1], comes[2], comes[3])


def split_hi_lo(value):
    hi = value.astype(BF16).astype(F32)
    return jnp.concatenate([hi, value - hi], axis=-1).astype(BF16)


def p_part_kernel(lbar, basis, out):
    gu = jnp.zeros((16, LANES), F32)
    for s in range(0, SHARDS, 2):
        left = jnp.concatenate(
            [lbar[16 * s : 16 * s + 16, :], lbar[16 * s + 16 : 16 * s + 32, :]], axis=1
        )
        right = basis[s : s + 2, 0:LANES, :].reshape(2 * LANES, LANES)
        gu = gu + jnp.dot(left, right, preferred_element_type=F32)
    tiles = lbar[GU_ROWS:BLOCK, :].astype(F32)
    dn = jnp.zeros((8, RANK), F32)
    for q in range(DN_TILES):
        right = basis[4 * q : 4 * q + 4, LANES:B_ROWS, :].astype(F32)
        right = jnp.concatenate([right[:, :, 0:RANK], right[:, :, RANK:LANES]], axis=1)
        dn = dn + jnp.dot(
            tiles[8 * q : 8 * q + 8].astype(BF16),
            right.reshape(LANES, RANK).astype(BF16),
            preferred_element_type=F32,
        )
    part = jnp.concatenate([gu[0:8, 0:RANK], gu[8:16, RANK:LANES], dn], axis=0)
    block = split_hi_lo(part)
    for rep in range(REPS):
        out[rep] = block


def p_part(lbar, basis):
    return pl.pallas_call(
        p_part_kernel,
        out_shape=jax.ShapeDtypeStruct((REPS, 24, LANES), BF16),
        in_specs=[VMEM, VMEM],
        out_specs=VMEM,
        compiler_params=params(16),
    )(lbar, basis)


def p_sum_kernel(ps, lbar, out):
    total = jnp.sum(ps[...].astype(F32), axis=0)
    rows = split_hi_lo(total[:, 0:RANK] + total[:, RANK:LANES]).astype(F32)
    tiles = lbar[GU_ROWS:BLOCK, :].astype(F32)
    for s in range(SHARDS):
        gu = lbar[16 * s : 16 * s + 16, :].astype(F32)
        dn = tiles[8 * (s // 4) : 8 * (s // 4) + 8]
        out[s] = jnp.concatenate([gu, dn, rows], axis=0).astype(BF16)


def p_sum(ps, lbar):
    return pl.pallas_call(
        p_sum_kernel,
        out_shape=jax.ShapeDtypeStruct((SHARDS, 48, LANES), BF16),
        in_specs=[VMEM, VMEM],
        out_specs=VMEM,
        compiler_params=params(16),
    )(ps, lbar)


def inverse_factors(grams):
    eye = (
        lax.broadcasted_iota(jnp.int32, (RANK, RANK), 0)
        == lax.broadcasted_iota(jnp.int32, (RANK, RANK), 1)
    ).astype(F32)
    sub = lax.broadcasted_iota(jnp.int32, (8, LANES), 0)

    def spread_lane(x, k):
        return jnp.broadcast_to(x[:, k : k + 1], (8, LANES))

    def spread_row(x, k):
        return jnp.broadcast_to(x[k : k + 1], (8, LANES))

    works = []
    for gram in grams:
        work = jnp.concatenate([gram, eye], axis=1)
        works.append([work[8 * b : 8 * b + 8] for b in range(8)])
    outs = [[] for _ in grams]
    for now in range(8):
        pivots = [jnp.ones((8, LANES), F32) for _ in grams]
        ratios, rows = [[] for _ in grams], [[] for _ in grams]
        spread = [[spread_lane(work[now], 8 * now + j) for j in range(8)] for work in works]
        for j in range(8):
            for m, work in enumerate(works):
                cols = spread[m]
                pivot = spread_row(cols[j], j)
                inverse = 1.0 / pivot
                pivots[m] = jnp.where(sub == j, pivot, pivots[m])
                rows[m].append(spread_row(work[now], j) * inverse)
                ratios[m].append([spread_row(cols[i], j) * inverse for i in range(j + 1, 8)])
                if j < 7:
                    below = jnp.where(sub > j, cols[j], 0.0)
                    for i in range(j + 1, 8):
                        cols[i] = cols[i] - below * ratios[m][j][i - j - 1]
                    work[now] = work[now] - below * rows[m][j]
        for m, work in enumerate(works):
            for b in range(now + 1, 8):
                cols = [spread_lane(work[b], 8 * now + j) for j in range(8)]
                for j in range(8):
                    for i in range(j + 1, 8):
                        cols[i] = cols[i] - cols[j] * ratios[m][j][i - j - 1]
                    work[b] = work[b] - cols[j] * rows[m][j]
            outs[m].append(work[now] * lax.rsqrt(pivots[m]))
    return [jnp.concatenate(out, axis=0)[:, RANK:LANES] for out in outs]


def exact_dot(a, b, dims):
    return lax.dot_general(
        a, b, (dims, ((), ())), precision=lax.Precision.HIGHEST, preferred_element_type=F32
    )


def factor_kernel(pos, recv, a_out, q_out, q_rows):
    block = recv[...].astype(F32)
    columns = [
        block[:, 8 * m : 8 * m + 8, :].reshape(256, LANES).astype(BF16) for m in range(3)
    ]
    left = block[:, 24:48, :]
    left = left[:, :, 0:RANK] + left[:, :, RANK:LANES]
    lefts = [left[:, 8 * m : 8 * m + 8, :].reshape(256, RANK) for m in range(3)]
    grams = [exact_dot(p, p, ((0,), (0,))) for p in lefts]
    inverses = inverse_factors(grams)
    hs = [exact_dot(p, v, ((1,), (1,))).astype(BF16) for p, v in zip(lefts, inverses)]
    recons, qs = [], []
    for h, column in zip(hs, columns):
        q = lax.dot_general(column, h, (((0,), (0,)), ((), ())), preferred_element_type=F32)
        q = (q * (1.0 / REPS)).astype(BF16)
        qs.append(q.astype(F32))
        recon = lax.dot_general(h, q, (((1,), (1,)), ((), ())), preferred_element_type=F32)
        recons.append(recon.reshape(SHARDS, 8, LANES))
    a_out[...] = jnp.concatenate(recons, axis=1).astype(BF16)
    q_rows[...] = qs[2]
    dn = q_rows[pl.ds(pl.multiple_of(32 * lax.rem(pos[2], 4), 32), 32), :]
    dn = jnp.concatenate([dn, jnp.zeros_like(dn)], axis=1)
    gu = jnp.concatenate(qs[:2], axis=1)
    q_out[...] = jnp.concatenate([gu, dn], axis=0).astype(BF16)


def factor(pos, recv):
    return pl.pallas_call(
        factor_kernel,
        out_shape=(
            jax.ShapeDtypeStruct((SHARDS, 24, LANES), BF16),
            jax.ShapeDtypeStruct((Q_ROWS, LANES), BF16),
        ),
        in_specs=[SMEM, VMEM],
        out_specs=(VMEM, VMEM),
        scratch_shapes=[pltpu.VMEM((LANES, RANK), F32)],
        compiler_params=params(32),
    )(pos, recv)


Q_ROWS = LANES + 32
PAYLOAD = BLOCK + Q_ROWS


def pack_kernel(rows, q, out):
    for s in range(SHARDS):
        out[16 * s : 16 * s + 16, :] = rows[s].astype(F32)[0:16].astype(BF16)
    for half in range(DN_TILES // 2):
        two = [rows[8 * half + 4 * k].astype(F32)[16:24] for k in range(2)]
        at = GU_ROWS + 16 * half
        out[at : at + 16, :] = jnp.concatenate(two, axis=0).astype(BF16)
    out[BLOCK:PAYLOAD, :] = q[...]


def pack(rows, q):
    return pl.pallas_call(
        pack_kernel,
        out_shape=jax.ShapeDtypeStruct((PAYLOAD, LANES), BF16),
        in_specs=[VMEM, VMEM],
        out_specs=VMEM,
        compiler_params=params(16),
    )(rows, q)


def finish_kernel(
    pos, b0, b1, b2, b3, b4, b5, b6, b7, gs, gf, ge, gm, ds, df, de, dm,
    gs_o, ge_o, gm_o, ds_o, de_o, dm_o, gb_o, db_o,
    gs_v, ge_v, gm_v, ds_v, de_v, dm_v, stage, q_full, q_dn,
    gs_i, gf_i, ge_i, gm_i, ds_i, df_i, de_i, dm_i, sems, sems_in,
):
    arrivals = []

    def bring(pairs, at):
        row = []
        for i, (src, dst) in enumerate(pairs):
            row.append(
                pltpu.make_async_copy(src.at[at], dst.at[at], sems_in.at[len(arrivals), i])
            )
            row[-1].start()
        arrivals.append(row)

    bounds = [first_tile(PER * g) * LANES for g in range(GROUPS + 1)]
    for g in range(GROUPS):
        bring(
            ((gs, gs_i), (gf, gf_i), (ge, ge_i), (gm, gm_i)),
            (slice(None), slice(None), pl.ds(bounds[g], bounds[g + 1] - bounds[g])),
        )
    bring(((ds, ds_i), (df, df_i), (de, de_i), (dm, dm_i)), (slice(None), slice(None)))
    y, core, mine = pos[0], pos[1], pos[2]
    for i, block in enumerate((b0, b1, b2, b3, b4, b5, b6, b7)):
        rep = 2 * lax.rem(y - i % 4 + 4, 4) + (core if i < 4 else 1 - core)
        stage[rep] = block[...]

    def outer(slow, fast, error, moment, recon):
        combined = slow - fast.astype(F32) + error.astype(F32)
        moment_next = 0.9 * moment + recon
        return (
            slow - 0.7 * (recon + 0.9 * moment_next),
            (combined - recon).astype(BF16),
            moment_next,
        )

    copies = []

    def send(pairs, at):
        for src, dst in pairs:
            copies.append(pltpu.make_async_copy(src.at[at], dst.at[at], sems.at[len(copies)]))
            copies[-1].start()

    lane = lane_ids()

    def gu_recon(rep, shard):
        return stage[rep, 16 * shard : 16 * shard + 16, :].astype(F32).reshape(2, 8, LANES)

    for g in range(GROUPS):
        for copy in arrivals[g]:
            copy.wait()
        for shard in range(PER * g, PER * (g + 1)):
            for j in range(first_tile(shard + 1) - first_tile(shard)):
                recon = gu_recon(j, shard)
                if j == 0 and offset(shard) > 0:
                    other = gu_recon(0 if has_ninth(shard - 1) else 7, shard - 1)
                    recon = jnp.where(lane[None] < offset(shard), other, recon)
                at = (slice(None), slice(None), pl.ds((first_tile(shard) + j) * LANES, LANES))
                gs_v[at], ge_v[at], gm_v[at] = outer(
                    gs_i[at], gf_i[at], ge_i[at], gm_i[at], recon
                )
        send(
            ((gs_v, gs_o), (ge_v, ge_o), (gm_v, gm_o)),
            (slice(None), slice(None), pl.ds(bounds[g], bounds[g + 1] - bounds[g])),
        )
    for copy in arrivals[GROUPS]:
        copy.wait()
    tiles = [stage[r, GU_ROWS:BLOCK, :].astype(F32) for r in range(REPS)]
    for shard in range(SHARDS):
        q, a = shard // 4, shard % 4
        for half in range(2):
            recon = None
            for k in range(4):
                piece = tiles[4 * half + k][8 * q : 8 * q + 8]
                if k != a:
                    piece = pltpu.roll(piece, 32 * (k - a) % LANES, 1)
                recon = piece if k == 0 else jnp.where(lane < 32 * k, recon, piece)
            at = (slice(None), pl.ds(DN_COLS * shard + LANES * half, LANES))
            ds_v[at], de_v[at], dm_v[at] = outer(ds_i[at], df_i[at], de_i[at], dm_i[at], recon)
    send(((ds_v, ds_o), (de_v, de_o), (dm_v, dm_o)), (slice(None), slice(None)))

    for r in range(REPS):
        block = stage[r, BLOCK:PAYLOAD, :].astype(F32)
        q_full[LANES * r : LANES * r + LANES, :] = block[0:LANES]
        if r == 0:
            q_full[8 * LANES : 9 * LANES, :] = block[0:LANES]
        q_dn[32 * r : 32 * r + 32, :] = block[LANES:Q_ROWS, 0:RANK]
    gb_o[...] = q_full[pl.ds(offset(mine), GU_COLS), :].astype(BF16)
    db_o[...] = q_dn[...].T.astype(BF16)
    for copy in copies:
        copy.wait()


def finish(pos, blocks, gs, gf, ge, gm, ds, df, de, dm):
    def like(a):
        return jax.ShapeDtypeStruct(a.shape, a.dtype)

    gu, dn = (2, 8, FF), (8, D)
    return pl.pallas_call(
        finish_kernel,
        out_shape=(
            like(gs), like(ge), like(gm), like(ds), like(de), like(dm),
            jax.ShapeDtypeStruct((GU_COLS, LANES), BF16),
            jax.ShapeDtypeStruct((RANK, DN_COLS), BF16),
        ),
        in_specs=[SMEM] + [VMEM] * 8 + [ANY] * 8,
        out_specs=(ANY,) * 6 + (VMEM, VMEM),
        scratch_shapes=[
            pltpu.VMEM(gu, F32),
            pltpu.VMEM(gu, BF16),
            pltpu.VMEM(gu, F32),
            pltpu.VMEM(dn, F32),
            pltpu.VMEM(dn, BF16),
            pltpu.VMEM(dn, F32),
            pltpu.VMEM((REPS, PAYLOAD, LANES), BF16),
            pltpu.VMEM((9 * LANES, LANES), F32),
            pltpu.VMEM((DN_COLS, RANK), F32),
            pltpu.VMEM(gu, F32),
            pltpu.VMEM(gu, BF16),
            pltpu.VMEM(gu, BF16),
            pltpu.VMEM(gu, F32),
            pltpu.VMEM(dn, F32),
            pltpu.VMEM(dn, BF16),
            pltpu.VMEM(dn, BF16),
            pltpu.VMEM(dn, F32),
            pltpu.SemaphoreType.DMA((3 * (GROUPS + 1),)),
            pltpu.SemaphoreType.DMA((GROUPS + 1, 4)),
        ],
        compiler_params=params(56),
    )(pos, *blocks, gs, gf, ge, gm, ds, df, de, dm)


def shift(value, axis, size, by):
    return lax.ppermute(value, axis, [(i, (i + by) % size) for i in range(size)])


def swap(value):
    return lax.ppermute(value, "core", [(0, 1), (1, 0)])


def exchange(value, axis):
    return lax.all_to_all(value, axis, 0, 0, tiled=False)


def on_device(
    gu_slow, gu_fast, gu_error, gu_moment, gu_basis, dn_slow, dn_fast, dn_error, dn_moment, dn_basis
):
    pos = jnp.stack([lax.axis_index("y"), lax.axis_index("core"), lax.axis_index(SHARD)])
    pos = pos.astype(jnp.int32)
    gu_fast, gu_error = gu_fast[0], gu_error[0]
    dn_fast, dn_error = dn_fast[0], dn_error[0]
    basis = exchange(basis_tiles(pos, gu_basis, dn_basis.T), SHARD)
    own, oth = lower(pos, gu_slow, gu_fast, gu_error, dn_slow, dn_fast, dn_error)
    came = swap(oth)
    pair = own.astype(F32) + came.astype(F32)
    sends = {by: pair[by].astype(BF16) for by in (2, 1, 3)}
    comes = {by: shift(sends[by], "y", 4, by) for by in (2, 1, 3)}
    lbar = y_sum(own, came, comes)
    parts = exchange(p_part(lbar, basis), ("y", "core"))
    recv = exchange(p_sum(parts, lbar), SHARD)
    a_blocks, q_block = factor(pos, recv)
    payload = pack(exchange(a_blocks, SHARD), q_block)
    mine = {0: payload}
    for by in (2, 1, 3):
        mine[by] = shift(payload, "y", 4, by)
    blocks = [mine[by] for by in range(4)]
    blocks = blocks + [swap(b) for b in blocks]
    gs, ge, gm, ds, de, dm, gb, db = finish(
        pos, blocks, gu_slow, gu_fast, gu_error, gu_moment, dn_slow, dn_fast, dn_error, dn_moment
    )
    return gs, ge[None], gm, gb, ds, de[None], dm, db.T


def solution(mesh):
    fine = Mesh(mesh.devices.reshape(4, 2, 8, 4), ("y", "core", "z", "x"))
    rep = ("y", "core")
    weights, shared = P(None, SHARD, None), P(SHARD, None)
    replica = P(rep, None, SHARD, None)
    dn_replica = P(rep, SHARD, None)
    return jax.shard_map(
        on_device,
        mesh=fine,
        in_specs=(
            weights, replica, replica, weights, shared,
            shared, dn_replica, dn_replica, shared, shared,
        ),
        out_specs=(
            weights, replica, weights, shared,
            shared, dn_replica, shared, shared,
        ),
        check_vma=False,
    )
```

```python
import functools

import jax
import jax.numpy as jnp
from jax import lax
from jax.experimental import pallas as pl
from jax.experimental.pallas import tpu as pltpu
from jax.sharding import Mesh
from jax.sharding import PartitionSpec as P

FF = 29568
D = 8192
SHARDS = 32
REPS = 8
GU_COLS = FF // SHARDS
DN_COLS = D // SHARDS
LANES = 128
TILES = FF // LANES
RANK = 64
F32 = jnp.float32
BF16 = jnp.bfloat16
SHARD = ("z", "x")
VMEM = pl.BlockSpec(memory_space=pltpu.VMEM)
HBM = pl.BlockSpec(memory_space=pltpu.HBM)
ANY = pl.BlockSpec(memory_space=pl.ANY)
GROUPS = 4
PER = SHARDS // GROUPS


LIGHT = pl.CostEstimate(flops=1, bytes_accessed=1, transcendentals=0)


def params(mib):
    return pltpu.CompilerParams(vmem_limit_bytes=mib * 2**20)


def first_tile(shard):
    return TILES * shard // SHARDS


def offset(shard):
    return GU_COLS * shard - LANES * first_tile(shard)


def has_ninth(shard):
    return offset(shard) > 8 * LANES - GU_COLS


def places():
    return lax.axis_index("y"), lax.axis_index("core"), lax.axis_index("z") * 4 + lax.axis_index("x")


def lane_ids():
    return lax.broadcasted_iota(jnp.int32, (8, LANES), 1)


def group_bounds():
    bounds = [0]
    for g in range(GROUPS):
        bounds.append(min(TILES, first_tile(PER * (g + 1)) + 1) * LANES)
    return bounds


GU_ROWS = SHARDS * 16
DN_TILES = D // REPS // LANES
BLOCK = GU_ROWS + DN_TILES * 8


def lower_kernel(gs, gf, ge, ds, df, de, own, oth, gsv, gfv, gev, dsv, dfv, dev, sems):
    y, core, _ = places()
    bounds = group_bounds()
    copies = []
    for g in range(GROUPS):
        a, n = bounds[g], bounds[g + 1] - bounds[g]
        c, m = DN_COLS * PER * g, DN_COLS * PER
        row = []
        for i, (src, dst) in enumerate(((gs, gsv), (gf, gfv), (ge, gev))):
            at = (slice(None), slice(None), pl.ds(a, n))
            row.append(pltpu.make_async_copy(src.at[at], dst.at[at], sems.at[g, i]))
        for i, (src, dst) in enumerate(((ds, dsv), (df, dfv), (de, dev))):
            at = (slice(None), pl.ds(c, m))
            row.append(pltpu.make_async_copy(src.at[at], dst.at[at], sems.at[g, 3 + i]))
        for copy in row:
            copy.start()
        copies.append(row)
    first = core == 0
    lane = lane_ids()
    slots = [lax.rem(yy - y + 4, 4) for yy in range(4)]

    def gu_tile(tile):
        at = (slice(None), slice(None), pl.ds(tile * LANES, LANES))
        return gsv[at] - gfv[at].astype(F32) + gev[at].astype(F32)

    for shard in range(SHARDS):
        if shard % PER == 0:
            for copy in copies[shard // PER]:
                copy.wait()
        tiles = [gu_tile(first_tile(shard) + j) for j in range(8)]
        if has_ninth(shard):
            tiles[0] = jnp.where(lane[None] < 24, gu_tile(first_tile(shard) + 8), tiles[0])
        for yy in range(4):
            one, two = (tiles[2 * yy + c].reshape(16, LANES) for c in range(2))
            at = slice(16 * shard, 16 * shard + 16)
            own[slots[yy], at] = jnp.where(first, one, two).astype(BF16)
            oth[slots[yy], at] = jnp.where(first, two, one).astype(BF16)
    for half in range(DN_TILES // 2):
        parts = [[None, None] for _ in range(REPS)]
        for k in range(2):
            wide = pl.ds(4 * DN_COLS * (2 * half + k), 4 * DN_COLS)
            dn = dsv[:, wide] - dfv[:, wide].astype(F32) + dev[:, wide].astype(F32)
            for r in range(REPS):
                tile = None
                for a in range(4):
                    at = DN_COLS * a + LANES * (r // 4)
                    piece = dn[:, at : at + LANES]
                    if a != r % 4:
                        piece = pltpu.roll(piece, 32 * (a - r % 4) % LANES, 1)
                    tile = piece if a == 0 else jnp.where(lane < 32 * a, tile, piece)
                parts[r][k] = tile
        for yy in range(4):
            one, two = (jnp.concatenate(parts[2 * yy + c], axis=0) for c in range(2))
            at = slice(GU_ROWS + 16 * half, GU_ROWS + 16 * half + 16)
            own[slots[yy], at] = jnp.where(first, one, two).astype(BF16)
            oth[slots[yy], at] = jnp.where(first, two, one).astype(BF16)


def lower(gs, gf, ge, ds, df, de):
    shape = jax.ShapeDtypeStruct((4, BLOCK, LANES), BF16)
    return pl.pallas_call(
        lower_kernel,
        out_shape=(shape, shape),
        in_specs=[HBM] * 6,
        out_specs=(VMEM, VMEM),
        scratch_shapes=[
            pltpu.VMEM((2, 8, FF), F32),
            pltpu.VMEM((2, 8, FF), BF16),
            pltpu.VMEM((2, 8, FF), BF16),
            pltpu.VMEM((8, D), F32),
            pltpu.VMEM((8, D), BF16),
            pltpu.VMEM((8, D), BF16),
            pltpu.SemaphoreType.DMA((GROUPS, 6)),
        ],
        compiler_params=params(59),
        cost_estimate=LIGHT,
    )(gs, gf, ge, ds, df, de)


B_ROWS = LANES + 16


def basis_kernel(gu_any, dn_any, out, rows, dn_rows, gu, dn_t, sems):
    y, core, shard = places()
    rep = 2 * y + core
    start = LANES - offset(shard)
    copies = [
        pltpu.make_async_copy(gu_any, gu, sems.at[0]),
        pltpu.make_async_copy(dn_any, dn_t, sems.at[1]),
    ]
    for copy in copies:
        copy.start()
    for copy in copies:
        copy.wait()
    rows[0:LANES, :] = jnp.zeros((LANES, LANES), F32)
    rows[LANES : LANES + GU_COLS, :] = gu[...].astype(F32)
    rows[LANES + GU_COLS :, :] = jnp.zeros((rows.shape[0] - LANES - GU_COLS, LANES), F32)
    tile = rows[pl.ds(start + LANES * rep, LANES), :]
    ninth = rows[pl.ds(start + LANES * 8, LANES), :]
    tile = tile + jnp.where(rep == 0, ninth, 0.0)
    dn_rows[...] = dn_t[...].astype(F32).T
    dn = dn_rows[pl.ds(pl.multiple_of(32 * rep, 32), 32), :]
    dn = jnp.concatenate([dn[0:16], dn[16:32]], axis=1)
    block = jnp.concatenate([tile, dn], axis=0).astype(BF16)
    for z in range(8):
        out[z] = block


def basis_tiles(gu, dn_t):
    return pl.pallas_call(
        basis_kernel,
        out_shape=jax.ShapeDtypeStruct((8, B_ROWS, LANES), BF16),
        in_specs=[HBM, HBM],
        out_specs=VMEM,
        scratch_shapes=[
            pltpu.VMEM((1280, LANES), F32),
            pltpu.VMEM((DN_COLS, RANK), F32),
            pltpu.VMEM((GU_COLS, LANES), BF16),
            pltpu.VMEM((RANK, DN_COLS), BF16),
            pltpu.SemaphoreType.DMA((2,)),
        ],
        compiler_params=params(59),
    )(gu, dn_t)


def pair_kernel(own, came, zero, one, two, three, own_v, came_v, sems):
    order = (2, 1, 3, 0)
    copies = []
    for k in order:
        row = []
        for i, (src, dst) in enumerate(((own, own_v), (came, came_v))):
            row.append(pltpu.make_async_copy(src.at[k], dst.at[k], sems.at[k, i]))
            row[-1].start()
        copies.append(row)
    outs = (zero, one, two, three)
    for k, row in zip(order, copies):
        for copy in row:
            copy.wait()
        for at in range(0, BLOCK, 64):
            rows = slice(at, at + 64)
            total = own_v[k, rows].astype(F32) + came_v[k, rows].astype(F32)
            outs[k][rows] = total.astype(outs[k].dtype)


def pair_sums(own, came):
    block = (BLOCK, LANES)
    return pl.pallas_call(
        pair_kernel,
        out_shape=(
            jax.ShapeDtypeStruct(block, F32),
            *[jax.ShapeDtypeStruct(block, BF16)] * 3,
        ),
        in_specs=[ANY] * 2,
        out_specs=(VMEM,) * 4,
        scratch_shapes=[
            pltpu.VMEM((4, BLOCK, LANES), BF16),
            pltpu.VMEM((4, BLOCK, LANES), BF16),
            pltpu.SemaphoreType.DMA((4, 2)),
        ],
        compiler_params=params(16),
        cost_estimate=LIGHT,
    )(own, came)


X_ROWS = 8 * 16 + DN_TILES * 8


def y_sum_kernel(zero, one, two, three, out, x0, x1, x2, x3):
    for at in range(0, BLOCK, 64):
        rows = slice(at, at + 64)
        total = zero[rows]
        for ref in (one, two, three):
            total = total + ref[rows].astype(F32)
        out[rows] = total.astype(BF16)
    x = lax.axis_index("x")
    for k, ref in enumerate((x0, x1, x2, x3)):
        to_x = lax.rem(x + k, 4)
        for z in range(8):
            at = pl.multiple_of(16 * (4 * z + to_x), 16)
            ref[16 * z : 16 * z + 16, :] = out[pl.ds(at, 16), :]
        ref[8 * 16 :, :] = out[GU_ROWS:BLOCK, :]


def y_sum(zero, comes):
    return pl.pallas_call(
        y_sum_kernel,
        out_shape=(
            jax.ShapeDtypeStruct((BLOCK, LANES), BF16),
            *[jax.ShapeDtypeStruct((X_ROWS, LANES), BF16)] * 4,
        ),
        in_specs=[VMEM] * 4,
        out_specs=(VMEM,) * 5,
        compiler_params=params(16),
    )(zero, comes[1], comes[2], comes[3])


def split_hi_lo(value):
    hi = value.astype(BF16).astype(F32)
    return jnp.concatenate([hi, value - hi], axis=-1).astype(BF16)


def p_part_kernel(l0, l1, l2, l3, basis, out, dn_rows):
    x = lax.axis_index("x")
    lefts = (l0, l1, l2, l3)
    gu = jnp.zeros((64, LANES), F32)
    for z in range(0, 8, 2):
        left = [
            jnp.concatenate([ref[16 * i : 16 * i + 16, :] for ref in lefts], axis=0)
            for i in (z, z + 1)
        ]
        right = basis[z : z + 2, 0:LANES, :].reshape(2 * LANES, LANES)
        gu = gu + jnp.dot(jnp.concatenate(left, axis=1), right, preferred_element_type=F32)
    dn_rows[...] = jnp.zeros_like(dn_rows)
    right = basis[:, LANES:B_ROWS, :].astype(F32)
    right = jnp.concatenate([right[:, :, 0:RANK], right[:, :, RANK:LANES]], axis=1)
    dn_rows[:, pl.ds(pl.multiple_of(32 * x, 32), 32), :] = right
    tiles = [ref[8 * 16 :, :].astype(F32) for ref in lefts]
    dn = jnp.zeros((32, RANK), F32)
    for q in range(DN_TILES):
        left = jnp.concatenate([tile[8 * q : 8 * q + 8] for tile in tiles], axis=0)
        dn = dn + jnp.dot(
            left.astype(BF16), dn_rows[q].astype(BF16), preferred_element_type=F32
        )
    for k in range(4):
        part = jnp.concatenate(
            [
                gu[16 * k : 16 * k + 8, 0:RANK],
                gu[16 * k + 8 : 16 * k + 16, RANK:LANES],
                dn[8 * k : 8 * k + 8],
            ],
            axis=0,
        )
        block = split_hi_lo(part)
        to_x = lax.rem(x - k + 4, 4)
        for rep in range(REPS):
            out[4 * rep + to_x] = block


def p_part(rows, basis):
    return pl.pallas_call(
        p_part_kernel,
        out_shape=jax.ShapeDtypeStruct((4 * REPS, 24, LANES), BF16),
        in_specs=[VMEM] * 5,
        out_specs=VMEM,
        scratch_shapes=[pltpu.VMEM((DN_TILES, LANES, RANK), F32)],
        compiler_params=params(16),
    )(*rows, basis)


def p_sum_kernel(ps, lbar, out):
    total = jnp.sum(ps[...].astype(F32), axis=0)
    rows = total[:, 0:RANK] + total[:, RANK:LANES]
    rows = jnp.concatenate(
        [jnp.concatenate([rows[0:8], rows[8:16]], axis=1),
         jnp.concatenate([rows[16:24], jnp.zeros((8, RANK), F32)], axis=1)],
        axis=0,
    )
    tiles = lbar[GU_ROWS:BLOCK, :].astype(F32)
    for s in range(SHARDS):
        gu = lbar[16 * s : 16 * s + 16, :].astype(F32)
        dn = tiles[8 * (s // 4) : 8 * (s // 4) + 8]
        out[s] = jnp.concatenate([gu, dn, rows], axis=0).astype(BF16)


def p_sum(ps, lbar):
    return pl.pallas_call(
        p_sum_kernel,
        out_shape=jax.ShapeDtypeStruct((SHARDS, 40, LANES), BF16),
        in_specs=[VMEM, VMEM],
        out_specs=VMEM,
        compiler_params=params(16),
    )(ps, lbar)


def inverse_factors(grams):
    eye = (
        lax.broadcasted_iota(jnp.int32, (RANK, RANK), 0)
        == lax.broadcasted_iota(jnp.int32, (RANK, RANK), 1)
    ).astype(F32)
    sub = lax.broadcasted_iota(jnp.int32, (8, LANES), 0)

    def spread_lane(x, k):
        return jnp.broadcast_to(x[:, k : k + 1], (8, LANES))

    def spread_row(x, k):
        return jnp.broadcast_to(x[k : k + 1], (8, LANES))

    works = []
    for gram in grams:
        work = jnp.concatenate([gram, eye], axis=1)
        works.append([work[8 * b : 8 * b + 8] for b in range(8)])
    outs = [[] for _ in grams]
    for now in range(8):
        pivots = [jnp.ones((8, LANES), F32) for _ in grams]
        ratios, rows = [[] for _ in grams], [[] for _ in grams]
        spread = [[spread_lane(work[now], 8 * now + j) for j in range(8)] for work in works]
        for j in range(8):
            for m, work in enumerate(works):
                cols = spread[m]
                pivot = spread_row(cols[j], j)
                inverse = 1.0 / pivot
                pivots[m] = jnp.where(sub == j, pivot, pivots[m])
                rows[m].append(spread_row(work[now], j) * inverse)
                ratios[m].append([spread_row(cols[i], j) * inverse for i in range(j + 1, 8)])
                if j < 7:
                    below = jnp.where(sub > j, cols[j], 0.0)
                    for i in range(j + 1, 8):
                        cols[i] = cols[i] - below * ratios[m][j][i - j - 1]
                    work[now] = work[now] - below * rows[m][j]
        for m, work in enumerate(works):
            for b in range(now + 1, 8):
                cols = [spread_lane(work[b], 8 * now + j) for j in range(8)]
                for j in range(8):
                    for i in range(j + 1, 8):
                        cols[i] = cols[i] - cols[j] * ratios[m][j][i - j - 1]
                    work[b] = work[b] - cols[j] * rows[m][j]
            outs[m].append(work[now] * lax.rsqrt(pivots[m]))
    return [jnp.concatenate(out, axis=0)[:, RANK:LANES] for out in outs]


def exact_dot(a, b, dims):
    return lax.dot_general(
        a, b, (dims, ((), ())), precision=lax.Precision.HIGHEST, preferred_element_type=F32
    )


def factor_kernel(recv, a_out, q_out, q_rows):
    block = recv[...].astype(F32)
    columns = [
        block[:, 8 * m : 8 * m + 8, :].reshape(256, LANES).astype(BF16) for m in range(3)
    ]
    lefts = [
        block[:, 24:32, 0:RANK], block[:, 24:32, RANK:LANES], block[:, 32:40, 0:RANK]
    ]
    lefts = [left.reshape(256, RANK) for left in lefts]
    grams = [exact_dot(p, p, ((0,), (0,))) for p in lefts]
    inverses = inverse_factors(grams)
    hs = [exact_dot(p, v, ((1,), (1,))).astype(BF16) for p, v in zip(lefts, inverses)]
    recons, qs = [], []
    for h, column in zip(hs, columns):
        q = lax.dot_general(column, h, (((0,), (0,)), ((), ())), preferred_element_type=F32)
        q = (q * (1.0 / REPS)).astype(BF16)
        qs.append(q.astype(F32))
        recon = lax.dot_general(h, q, (((1,), (1,)), ((), ())), preferred_element_type=F32)
        recons.append(recon.reshape(SHARDS, 8, LANES))
    a_out[...] = jnp.concatenate(recons, axis=1).astype(BF16)
    q_rows[...] = qs[2]
    dn = q_rows[pl.ds(pl.multiple_of(32 * lax.axis_index("x"), 32), 32), :]
    dn = jnp.concatenate([dn, jnp.zeros_like(dn)], axis=1)
    gu = jnp.concatenate(qs[:2], axis=1)
    q_out[...] = jnp.concatenate([gu, dn], axis=0).astype(BF16)


def factor(recv):
    return pl.pallas_call(
        factor_kernel,
        out_shape=(
            jax.ShapeDtypeStruct((SHARDS, 24, LANES), BF16),
            jax.ShapeDtypeStruct((Q_ROWS, LANES), BF16),
        ),
        in_specs=[VMEM],
        out_specs=(VMEM, VMEM),
        scratch_shapes=[pltpu.VMEM((LANES, RANK), F32)],
        compiler_params=params(32),
    )(recv)


Q_ROWS = LANES + 32
PAYLOAD = BLOCK + Q_ROWS


def pack_kernel(rows, q, out):
    for s in range(SHARDS):
        out[16 * s : 16 * s + 16, :] = rows[s].astype(F32)[0:16].astype(BF16)
    for half in range(DN_TILES // 2):
        two = [rows[8 * half + 4 * k].astype(F32)[16:24] for k in range(2)]
        at = GU_ROWS + 16 * half
        out[at : at + 16, :] = jnp.concatenate(two, axis=0).astype(BF16)
    out[BLOCK:PAYLOAD, :] = q[...]


def pack(rows, q):
    return pl.pallas_call(
        pack_kernel,
        out_shape=jax.ShapeDtypeStruct((PAYLOAD, LANES), BF16),
        in_specs=[VMEM, VMEM],
        out_specs=VMEM,
        compiler_params=params(16),
    )(rows, q)


def finish_kernel(
    b0, b1, b2, b3, b4, b5, b6, b7, gs, gc, gm, ds, dc, dm,
    gs_o, ge_o, gm_o, ds_o, de_o, dm_o, gb_o, db_o,
    gs_v, ge_v, gm_v, ds_v, de_v, dm_v, stage, q_full, q_dn, sems,
):
    bounds = [first_tile(PER * g) * LANES for g in range(GROUPS + 1)]
    y, core, mine = places()
    for i, block in enumerate((b0, b1, b2, b3, b4, b5, b6, b7)):
        rep = 2 * lax.rem(y - i % 4 + 4, 4) + (core if i < 4 else 1 - core)
        stage[rep] = block[...]

    copies = []

    def send(pairs, at):
        for src, dst in pairs:
            copies.append(pltpu.make_async_copy(src.at[at], dst.at[at], sems.at[len(copies)]))
            copies[-1].start()

    lane = lane_ids()

    def gu_recon(rep, shard):
        return stage[rep, 16 * shard : 16 * shard + 16, :].astype(F32).reshape(2, 8, LANES)

    for g in range(GROUPS):
        for shard in range(PER * g, PER * (g + 1)):
            for j in range(first_tile(shard + 1) - first_tile(shard)):
                recon = gu_recon(j, shard)
                if j == 0 and offset(shard) > 0:
                    other = gu_recon(0 if has_ninth(shard - 1) else 7, shard - 1)
                    recon = jnp.where(lane[None] < offset(shard), other, recon)
                at = (slice(None), slice(None), pl.ds((first_tile(shard) + j) * LANES, LANES))
                gs_v[at] = gs[at] - SLOW_GAIN * recon
                ge_v[at] = (gc[at] - recon).astype(BF16)
                gm_v[at] = gm[at] + recon
        send(
            ((gs_v, gs_o), (ge_v, ge_o), (gm_v, gm_o)),
            (slice(None), slice(None), pl.ds(bounds[g], bounds[g + 1] - bounds[g])),
        )
    tiles = [stage[r, GU_ROWS:BLOCK, :].astype(F32) for r in range(REPS)]
    for shard in range(SHARDS):
        q, a = shard // 4, shard % 4
        for half in range(2):
            recon = None
            for k in range(4):
                piece = tiles[4 * half + k][8 * q : 8 * q + 8]
                if k != a:
                    piece = pltpu.roll(piece, 32 * (k - a) % LANES, 1)
                recon = piece if k == 0 else jnp.where(lane < 32 * k, recon, piece)
            at = (slice(None), pl.ds(DN_COLS * shard + LANES * half, LANES))
            ds_v[at] = ds[at] - SLOW_GAIN * recon
            de_v[at] = (dc[at] - recon).astype(BF16)
            dm_v[at] = dm[at] + recon
    send(((ds_v, ds_o), (de_v, de_o), (dm_v, dm_o)), (slice(None), slice(None)))

    for r in range(REPS):
        block = stage[r, BLOCK:PAYLOAD, :].astype(F32)
        q_full[LANES * r : LANES * r + LANES, :] = block[0:LANES]
        if r == 0:
            q_full[8 * LANES : 9 * LANES, :] = block[0:LANES]
        q_dn[32 * r : 32 * r + 32, :] = block[LANES:Q_ROWS, 0:RANK]
    gb_o[...] = q_full[pl.ds(offset(mine), GU_COLS), :].astype(BF16)
    db_o[...] = q_dn[...].T.astype(BF16)
    for copy in copies:
        copy.wait()


def finish(blocks, parts, dn_parts):
    gu, dn = (2, 8, FF), (8, D)
    kinds = (F32, BF16, F32)
    return pl.pallas_call(
        finish_kernel,
        out_shape=(
            *[jax.ShapeDtypeStruct(gu, kind) for kind in kinds],
            *[jax.ShapeDtypeStruct(dn, kind) for kind in kinds],
            jax.ShapeDtypeStruct((GU_COLS, LANES), BF16),
            jax.ShapeDtypeStruct((RANK, DN_COLS), BF16),
        ),
        in_specs=[VMEM] * 14,
        out_specs=(ANY,) * 6 + (VMEM, VMEM),
        scratch_shapes=[
            *[pltpu.VMEM(gu, kind) for kind in kinds],
            *[pltpu.VMEM(dn, kind) for kind in kinds],
            pltpu.VMEM((REPS, PAYLOAD, LANES), BF16),
            pltpu.VMEM((9 * LANES, LANES), F32),
            pltpu.VMEM((DN_COLS, RANK), F32),
            pltpu.SemaphoreType.DMA((3 * (GROUPS + 1),)),
        ],
        compiler_params=params(32),
    )(*blocks, *parts, *dn_parts)


MOMENT_GAIN = 0.7 * 0.9 * 0.9
SLOW_GAIN = 0.7 * 1.9


def settled(slow, fast, error, moment):
    combined = slow - fast.astype(F32) + error.astype(F32)
    return slow - MOMENT_GAIN * moment, combined, 0.9 * moment


def shift(value, axis, size, by):
    return lax.ppermute(value, axis, [(i, (i + by) % size) for i in range(size)])


def swap(value):
    return lax.ppermute(value, "core", [(0, 1), (1, 0)])


def exchange(value, axis):
    return lax.all_to_all(value, axis, 0, 0, tiled=False)


def on_device(
    gu_slow, gu_fast, gu_error, gu_moment, gu_basis, dn_slow, dn_fast, dn_error, dn_moment, dn_basis
):
    gu_fast, gu_error = gu_fast[0], gu_error[0]
    dn_fast, dn_error = dn_fast[0], dn_error[0]
    basis = exchange(basis_tiles(gu_basis, dn_basis.T), "z")
    own, oth = lower(gu_slow, gu_fast, gu_error, dn_slow, dn_fast, dn_error)
    came = swap(oth)
    zero, *sends = pair_sums(own, came)
    comes = {by: shift(sends[by - 1], "y", 4, by) for by in (2, 1, 3)}
    lbar, *rows = y_sum(zero, comes)
    for by in (2, 1, 3):
        rows[by] = shift(rows[by], "x", 4, by)
    parts = exchange(p_part(rows, basis), ("y", "core", "x"))
    recv = exchange(p_sum(parts, lbar), SHARD)
    a_blocks, q_block = factor(recv)
    payload = pack(exchange(a_blocks, SHARD), q_block)
    mine = {0: payload}
    for by in (2, 1, 3):
        mine[by] = shift(payload, "y", 4, by)
    blocks = [mine[by] for by in range(4)]
    blocks = blocks + [swap(b) for b in blocks]
    gs, ge, gm, ds, de, dm, gb, db = finish(
        blocks,
        settled(gu_slow, gu_fast, gu_error, gu_moment),
        settled(dn_slow, dn_fast, dn_error, dn_moment),
    )
    return gs, ge[None], gm, gb, ds, de[None], dm, db.T


def solution(mesh):
    fine = Mesh(mesh.devices.reshape(4, 2, 8, 4), ("y", "core", "z", "x"))
    rep = ("y", "core")
    weights, shared = P(None, SHARD, None), P(SHARD, None)
    replica = P(rep, None, SHARD, None)
    dn_replica = P(rep, SHARD, None)
    return jax.shard_map(
        on_device,
        mesh=fine,
        in_specs=(
            weights, replica, replica, weights, shared,
            shared, dn_replica, dn_replica, shared, shared,
        ),
        out_specs=(
            weights, replica, weights, shared,
            shared, dn_replica, shared, shared,
        ),
        check_vma=False,
    )
```

```python
import functools

import jax
import jax.numpy as jnp
from jax import lax
from jax.experimental import pallas as pl
from jax.experimental.pallas import tpu as pltpu
from jax.sharding import Mesh
from jax.sharding import PartitionSpec as P

FF = 29568
D = 8192
SHARDS = 32
REPS = 8
GU_COLS = FF // SHARDS
DN_COLS = D // SHARDS
LANES = 128
TILES = FF // LANES
RANK = 64
F32 = jnp.float32
BF16 = jnp.bfloat16
SHARD = ("z", "x")
VMEM = pl.BlockSpec(memory_space=pltpu.VMEM)
HBM = pl.BlockSpec(memory_space=pltpu.HBM)
ANY = pl.BlockSpec(memory_space=pl.ANY)
GROUPS = 4
PER = SHARDS // GROUPS


LIGHT = pl.CostEstimate(flops=1, bytes_accessed=1, transcendentals=0)


def params(mib):
    return pltpu.CompilerParams(vmem_limit_bytes=mib * 2**20)


def first_tile(shard):
    return TILES * shard // SHARDS


def offset(shard):
    return GU_COLS * shard - LANES * first_tile(shard)


def has_ninth(shard):
    return offset(shard) > 8 * LANES - GU_COLS


def places():
    return lax.axis_index("y"), lax.axis_index("core"), lax.axis_index("z") * 4 + lax.axis_index("x")


def lane_ids():
    return lax.broadcasted_iota(jnp.int32, (8, LANES), 1)


def group_bounds():
    bounds = [0]
    for g in range(GROUPS):
        bounds.append(min(TILES, first_tile(PER * (g + 1)) + 1) * LANES)
    return bounds


GU_ROWS = SHARDS * 16
DN_TILES = D // REPS // LANES
BLOCK = GU_ROWS + DN_TILES * 8
X_ROWS = 8 * 16 + 16


def lower_kernel(gs, gf, ge, ds, df, de, own, oth, gsv, gfv, gev, dsv, dfv, dev, sems):
    core = lax.axis_index("core")
    bounds = group_bounds()
    copies = []
    for g in range(GROUPS):
        a, n = bounds[g], bounds[g + 1] - bounds[g]
        c, m = DN_COLS * PER * g, DN_COLS * PER
        row = []
        for i, (src, dst) in enumerate(((gs, gsv), (gf, gfv), (ge, gev))):
            at = (slice(None), slice(None), pl.ds(a, n))
            row.append(pltpu.make_async_copy(src.at[at], dst.at[at], sems.at[g, i]))
        for i, (src, dst) in enumerate(((ds, dsv), (df, dfv), (de, dev))):
            at = (slice(None), pl.ds(c, m))
            row.append(pltpu.make_async_copy(src.at[at], dst.at[at], sems.at[g, 3 + i]))
        for copy in row:
            copy.start()
        copies.append(row)
    first = core == 0
    lane = lane_ids()

    def gu_tile(tile):
        at = (slice(None), slice(None), pl.ds(tile * LANES, LANES))
        return gsv[at] - gfv[at].astype(F32) + gev[at].astype(F32)

    def put(yy, x, at, one, two):
        own[4 * yy + x, at : at + 16] = jnp.where(first, one, two).astype(BF16)
        oth[4 * yy + x, at : at + 16] = jnp.where(first, two, one).astype(BF16)

    for shard in range(SHARDS):
        if shard % PER == 0:
            for copy in copies[shard // PER]:
                copy.wait()
        tiles = [gu_tile(first_tile(shard) + j) for j in range(8)]
        if has_ninth(shard):
            tiles[0] = jnp.where(lane[None] < 24, gu_tile(first_tile(shard) + 8), tiles[0])
        for yy in range(4):
            one, two = (tiles[2 * yy + c].reshape(16, LANES) for c in range(2))
            put(yy, shard % 4, 16 * (shard // 4), one, two)
    for x in range(4):
        parts = [[None, None] for _ in range(REPS)]
        for p in range(2):
            sources = []
            for j in range(4):
                at = (slice(None), pl.ds(DN_COLS * (4 * (4 * p + j) + x), DN_COLS))
                sources.append(dsv[at] - dfv[at].astype(F32) + dev[at].astype(F32))
            for r in range(REPS):
                tile = None
                for j in range(4):
                    at = LANES * (r // 4)
                    piece = sources[j][:, at : at + LANES]
                    if j != r % 4:
                        piece = pltpu.roll(piece, 32 * (j - r % 4) % LANES, 1)
                    tile = piece if j == 0 else jnp.where(lane < 32 * j, tile, piece)
                parts[r][p] = tile
        for yy in range(4):
            one, two = (jnp.concatenate(parts[2 * yy + c], axis=0) for c in range(2))
            put(yy, x, 8 * 16, one, two)


def lower(gs, gf, ge, ds, df, de):
    shape = jax.ShapeDtypeStruct((16, X_ROWS, LANES), BF16)
    return pl.pallas_call(
        lower_kernel,
        out_shape=(shape, shape),
        in_specs=[HBM] * 6,
        out_specs=(VMEM, VMEM),
        scratch_shapes=[
            pltpu.VMEM((2, 8, FF), F32),
            pltpu.VMEM((2, 8, FF), BF16),
            pltpu.VMEM((2, 8, FF), BF16),
            pltpu.VMEM((8, D), F32),
            pltpu.VMEM((8, D), BF16),
            pltpu.VMEM((8, D), BF16),
            pltpu.SemaphoreType.DMA((GROUPS, 6)),
        ],
        compiler_params=params(54),
        cost_estimate=LIGHT,
    )(gs, gf, ge, ds, df, de)


B_ROWS = LANES + 16


def basis_kernel(gu_any, dn_any, out, rows, dn_rows, gu, dn_t, sems):
    y, core, shard = places()
    rep = 2 * y + core
    start = LANES - offset(shard)
    copies = [
        pltpu.make_async_copy(gu_any, gu, sems.at[0]),
        pltpu.make_async_copy(dn_any, dn_t, sems.at[1]),
    ]
    for copy in copies:
        copy.start()
    for copy in copies:
        copy.wait()
    rows[0:LANES, :] = jnp.zeros((LANES, LANES), F32)
    rows[LANES : LANES + GU_COLS, :] = gu[...].astype(F32)
    rows[LANES + GU_COLS :, :] = jnp.zeros((rows.shape[0] - LANES - GU_COLS, LANES), F32)
    tile = rows[pl.ds(start + LANES * rep, LANES), :]
    ninth = rows[pl.ds(start + LANES * 8, LANES), :]
    tile = tile + jnp.where(rep == 0, ninth, 0.0)
    dn_rows[...] = dn_t[...].astype(F32).T
    dn = dn_rows[pl.ds(pl.multiple_of(32 * rep, 32), 32), :]
    dn = jnp.concatenate([dn[0:16], dn[16:32]], axis=1)
    block = jnp.concatenate([tile, dn], axis=0).astype(BF16)
    for z in range(8):
        out[z] = block


def basis_tiles(gu, dn_t):
    return pl.pallas_call(
        basis_kernel,
        out_shape=jax.ShapeDtypeStruct((8, B_ROWS, LANES), BF16),
        in_specs=[HBM, HBM],
        out_specs=VMEM,
        scratch_shapes=[
            pltpu.VMEM((1280, LANES), F32),
            pltpu.VMEM((DN_COLS, RANK), F32),
            pltpu.VMEM((GU_COLS, LANES), BF16),
            pltpu.VMEM((RANK, DN_COLS), BF16),
            pltpu.SemaphoreType.DMA((2,)),
        ],
        compiler_params=params(16),
    )(gu, dn_t)


def pair_kernel(own, came, zero, one, two, three):
    y = lax.axis_index("y")
    for k, out in ((2, two), (1, one), (3, three), (0, zero)):
        to = 4 * lax.rem(y + k, 4)
        for x in range(4):
            total = own[to + x].astype(F32) + came[to + x].astype(F32)
            out[x] = total.astype(out.dtype)


def pair_sums(own, came):
    block = (4, X_ROWS, LANES)
    return pl.pallas_call(
        pair_kernel,
        out_shape=(
            jax.ShapeDtypeStruct(block, F32),
            *[jax.ShapeDtypeStruct(block, BF16)] * 3,
        ),
        in_specs=[VMEM] * 2,
        out_specs=(VMEM,) * 4,
        compiler_params=params(16),
        cost_estimate=LIGHT,
    )(own, came)


def y_sum_kernel(zero, one, two, three, x0, x1, x2, x3, sums):
    for x in range(4):
        total = zero[x]
        for ref in (one, two, three):
            total = total + ref[x].astype(F32)
        sums[x] = total.astype(BF16)
    x = lax.axis_index("x")
    for k, ref in enumerate((x0, x1, x2, x3)):
        ref[...] = sums[lax.rem(x + k, 4)]


def y_sum(zero, comes):
    return pl.pallas_call(
        y_sum_kernel,
        out_shape=(jax.ShapeDtypeStruct((X_ROWS, LANES), BF16),) * 4,
        in_specs=[VMEM] * 4,
        out_specs=(VMEM,) * 4,
        scratch_shapes=[pltpu.VMEM((4, X_ROWS, LANES), BF16)],
        compiler_params=params(16),
    )(zero, comes[1], comes[2], comes[3])


P_ROWS = 48
Z_ROWS = 4 * 24 + P_ROWS


def p_part_kernel(l0, l1, l2, l3, basis, rows, out, stage):
    x = lax.axis_index("x")
    for k, ref in enumerate((l0, l1, l2, l3)):
        stage[lax.rem(x - k + 4, 4)] = ref[...]
    lows = [stage[x] for x in range(4)]
    sums = [stage[x, 8 * 16 : X_ROWS, :].astype(F32) for x in range(4)]
    gu = jnp.zeros((64, LANES), F32)
    for z in range(0, 8, 2):
        left = [
            jnp.concatenate([low[16 * i : 16 * i + 16] for low in lows], axis=0)
            for i in (z, z + 1)
        ]
        rows[z, 0:64, :] = left[0]
        rows[z + 1, 0:64, :] = left[1]
        right = basis[z : z + 2, 0:LANES, :].reshape(2 * LANES, LANES)
        gu = gu + jnp.dot(jnp.concatenate(left, axis=1), right, preferred_element_type=F32)
    dn = jnp.zeros((32, RANK), F32)
    for p in range(2):
        left = [total[8 * p : 8 * p + 8] for total in sums]
        left = jnp.concatenate(left, axis=0).astype(BF16)
        for z in range(4 * p, 4 * p + 4):
            rows[z, 64:96, :] = left
        right = basis[4 * p : 4 * p + 4, LANES:B_ROWS, :].astype(F32)
        right = jnp.concatenate([right[:, :, 0:RANK], right[:, :, RANK:LANES]], axis=1)
        right = right.reshape(LANES, RANK).astype(BF16)
        dn = dn + jnp.dot(left, right, preferred_element_type=F32)
    parts = [
        jnp.concatenate(
            [
                gu[16 * x : 16 * x + 8, 0:RANK],
                gu[16 * x + 8 : 16 * x + 16, RANK:LANES],
                dn[8 * x : 8 * x + 8],
            ],
            axis=0,
        )
        for x in range(4)
    ]
    block = jnp.concatenate(
        [jnp.concatenate(parts[k : k + 2], axis=1) for k in (0, 2)], axis=0
    ).astype(BF16)
    for member in range(32):
        out[member] = block


def p_part(rows, basis):
    return pl.pallas_call(
        p_part_kernel,
        out_shape=(
            jax.ShapeDtypeStruct((8, 96, LANES), BF16),
            jax.ShapeDtypeStruct((32, P_ROWS, LANES), BF16),
        ),
        in_specs=[VMEM] * 5,
        out_specs=(VMEM,) * 2,
        scratch_shapes=[pltpu.VMEM((4, X_ROWS, LANES), BF16)],
        compiler_params=params(16),
    )(*rows, basis)


def p_sum_kernel(ps, rows, out):
    total = jnp.sum(ps[...].astype(F32), axis=0).astype(BF16)
    for z in range(8):
        out[z, 0:96, :] = rows[z]
        out[z, 96:Z_ROWS, :] = total


def p_sum(ps, rows):
    return pl.pallas_call(
        p_sum_kernel,
        out_shape=jax.ShapeDtypeStruct((8, Z_ROWS, LANES), BF16),
        in_specs=[VMEM, VMEM],
        out_specs=VMEM,
        compiler_params=params(16),
    )(ps, rows)


def inverse_factors(grams):
    eye = (
        lax.broadcasted_iota(jnp.int32, (RANK, RANK), 0)
        == lax.broadcasted_iota(jnp.int32, (RANK, RANK), 1)
    ).astype(F32)
    sub = lax.broadcasted_iota(jnp.int32, (8, LANES), 0)

    def spread_lane(x, k):
        return jnp.broadcast_to(x[:, k : k + 1], (8, LANES))

    def spread_row(x, k):
        return jnp.broadcast_to(x[k : k + 1], (8, LANES))

    works = []
    for gram in grams:
        work = jnp.concatenate([gram, eye], axis=1)
        works.append([work[8 * b : 8 * b + 8] for b in range(8)])
    outs = [[] for _ in grams]
    for now in range(8):
        pivots = [jnp.ones((8, LANES), F32) for _ in grams]
        ratios, rows = [[] for _ in grams], [[] for _ in grams]
        spread = [[spread_lane(work[now], 8 * now + j) for j in range(8)] for work in works]
        for j in range(8):
            for m, work in enumerate(works):
                cols = spread[m]
                pivot = spread_row(cols[j], j)
                inverse = 1.0 / pivot
                pivots[m] = jnp.where(sub == j, pivot, pivots[m])
                rows[m].append(spread_row(work[now], j) * inverse)
                ratios[m].append([spread_row(cols[i], j) * inverse for i in range(j + 1, 8)])
                if j < 7:
                    below = jnp.where(sub > j, cols[j], 0.0)
                    for i in range(j + 1, 8):
                        cols[i] = cols[i] - below * ratios[m][j][i - j - 1]
                    work[now] = work[now] - below * rows[m][j]
        for m, work in enumerate(works):
            for b in range(now + 1, 8):
                cols = [spread_lane(work[b], 8 * now + j) for j in range(8)]
                for j in range(8):
                    for i in range(j + 1, 8):
                        cols[i] = cols[i] - cols[j] * ratios[m][j][i - j - 1]
                    work[b] = work[b] - cols[j] * rows[m][j]
            outs[m].append(work[now] * lax.rsqrt(pivots[m]))
    return [jnp.concatenate(out, axis=0)[:, RANK:LANES] for out in outs]


def exact_dot(a, b, dims):
    return lax.dot_general(
        a, b, (dims, ((), ())), precision=lax.Precision.HIGHEST, preferred_element_type=F32
    )


def factor_kernel(recv, a_out, q_out, q_rows):
    block = recv[...].astype(F32)
    gu = block[:, 0:64, :].reshape(8, 4, 16, LANES)
    columns = [gu[:, :, 0:8], gu[:, :, 8:16], block[:, 64:96, :]]
    columns = [column.reshape(256, LANES).astype(BF16) for column in columns]
    lefts = []
    for m in range(3):
        left = [
            block[:, at : at + 8, RANK * b : RANK * b + RANK]
            for at in (96 + 8 * m, 120 + 8 * m)
            for b in range(2)
        ]
        lefts.append(jnp.stack(left, axis=1).reshape(256, RANK))
    grams = [exact_dot(p, p, ((0,), (0,))) for p in lefts]
    inverses = inverse_factors(grams)
    hs = [exact_dot(p, v, ((1,), (1,))).astype(BF16) for p, v in zip(lefts, inverses)]
    recons, qs = [], []
    for h, column in zip(hs, columns):
        q = lax.dot_general(column, h, (((0,), (0,)), ((), ())), preferred_element_type=F32)
        q = (q * (1.0 / REPS)).astype(BF16)
        qs.append(q.astype(F32))
        recon = lax.dot_general(h, q, (((1,), (1,)), ((), ())), preferred_element_type=F32)
        recons.append(recon.reshape(SHARDS, 8, LANES))
    a_out[...] = jnp.concatenate(recons, axis=1).astype(BF16)
    q_rows[...] = qs[2]
    dn = q_rows[pl.ds(pl.multiple_of(32 * lax.rem(lax.axis_index("z"), 4), 32), 32), :]
    dn = jnp.concatenate([dn, jnp.zeros_like(dn)], axis=1)
    gu = jnp.concatenate(qs[:2], axis=1)
    q_out[...] = jnp.concatenate([gu, dn], axis=0).astype(BF16)


def factor(recv):
    return pl.pallas_call(
        factor_kernel,
        out_shape=(
            jax.ShapeDtypeStruct((SHARDS, 24, LANES), BF16),
            jax.ShapeDtypeStruct((Q_ROWS, LANES), BF16),
        ),
        in_specs=[VMEM],
        out_specs=(VMEM, VMEM),
        scratch_shapes=[pltpu.VMEM((LANES, RANK), F32)],
        compiler_params=params(32),
    )(recv)


Q_ROWS = LANES + 32
PAYLOAD = BLOCK + Q_ROWS


def pack_kernel(rows, q, out):
    for s in range(SHARDS):
        out[16 * s : 16 * s + 16, :] = rows[s].astype(F32)[0:16].astype(BF16)
    for x in range(4):
        two = [rows[16 * p + x].astype(F32)[16:24] for p in range(2)]
        at = GU_ROWS + 16 * x
        out[at : at + 16, :] = jnp.concatenate(two, axis=0).astype(BF16)
    out[BLOCK:PAYLOAD, :] = q[...]


def pack(rows, q):
    return pl.pallas_call(
        pack_kernel,
        out_shape=jax.ShapeDtypeStruct((PAYLOAD, LANES), BF16),
        in_specs=[VMEM, VMEM],
        out_specs=VMEM,
        compiler_params=params(16),
    )(rows, q)


def finish_kernel(
    b0, b1, b2, b3, b4, b5, b6, b7, gs, gc, gm, ds, dc, dm,
    gs_o, ge_o, gm_o, ds_o, de_o, dm_o, gb_o, db_o,
    gs_v, ge_v, gm_v, ds_v, de_v, dm_v, stage, q_full, q_dn, sems,
):
    bounds = [first_tile(PER * g) * LANES for g in range(GROUPS + 1)]
    y, core, mine = places()
    for i, block in enumerate((b0, b1, b2, b3, b4, b5, b6, b7)):
        rep = 2 * lax.rem(y - i % 4 + 4, 4) + (core if i < 4 else 1 - core)
        stage[rep] = block[...]

    copies = []

    def send(pairs, at):
        for src, dst in pairs:
            copies.append(pltpu.make_async_copy(src.at[at], dst.at[at], sems.at[len(copies)]))
            copies[-1].start()

    lane = lane_ids()

    def gu_recon(rep, shard):
        return stage[rep, 16 * shard : 16 * shard + 16, :].astype(F32).reshape(2, 8, LANES)

    for g in range(GROUPS):
        for shard in range(PER * g, PER * (g + 1)):
            for j in range(first_tile(shard + 1) - first_tile(shard)):
                recon = gu_recon(j, shard)
                if j == 0 and offset(shard) > 0:
                    other = gu_recon(0 if has_ninth(shard - 1) else 7, shard - 1)
                    recon = jnp.where(lane[None] < offset(shard), other, recon)
                at = (slice(None), slice(None), pl.ds((first_tile(shard) + j) * LANES, LANES))
                gs_v[at] = gs[at] - SLOW_GAIN * recon
                ge_v[at] = (gc[at] - recon).astype(BF16)
                gm_v[at] = gm[at] + recon
        send(
            ((gs_v, gs_o), (ge_v, ge_o), (gm_v, gm_o)),
            (slice(None), slice(None), pl.ds(bounds[g], bounds[g + 1] - bounds[g])),
        )
    tiles = [stage[r, GU_ROWS:BLOCK, :].astype(F32) for r in range(REPS)]
    for shard in range(SHARDS):
        z, x = shard // 4, shard % 4
        q, a = 2 * x + z // 4, z % 4
        for half in range(2):
            recon = None
            for k in range(4):
                piece = tiles[4 * half + k][8 * q : 8 * q + 8]
                if k != a:
                    piece = pltpu.roll(piece, 32 * (k - a) % LANES, 1)
                recon = piece if k == 0 else jnp.where(lane < 32 * k, recon, piece)
            at = (slice(None), pl.ds(DN_COLS * shard + LANES * half, LANES))
            ds_v[at] = ds[at] - SLOW_GAIN * recon
            de_v[at] = (dc[at] - recon).astype(BF16)
            dm_v[at] = dm[at] + recon
    send(((ds_v, ds_o), (de_v, de_o), (dm_v, dm_o)), (slice(None), slice(None)))

    for r in range(REPS):
        block = stage[r, BLOCK:PAYLOAD, :].astype(F32)
        q_full[LANES * r : LANES * r + LANES, :] = block[0:LANES]
        if r == 0:
            q_full[8 * LANES : 9 * LANES, :] = block[0:LANES]
        q_dn[32 * r : 32 * r + 32, :] = block[LANES:Q_ROWS, 0:RANK]
    gb_o[...] = q_full[pl.ds(offset(mine), GU_COLS), :].astype(BF16)
    db_o[...] = q_dn[...].T.astype(BF16)
    for copy in copies:
        copy.wait()


def finish(blocks, parts, dn_parts):
    gu, dn = (2, 8, FF), (8, D)
    kinds = (F32, BF16, F32)
    return pl.pallas_call(
        finish_kernel,
        out_shape=(
            *[jax.ShapeDtypeStruct(gu, kind) for kind in kinds],
            *[jax.ShapeDtypeStruct(dn, kind) for kind in kinds],
            jax.ShapeDtypeStruct((GU_COLS, LANES), BF16),
            jax.ShapeDtypeStruct((RANK, DN_COLS), BF16),
        ),
        in_specs=[VMEM] * 14,
        out_specs=(ANY,) * 6 + (VMEM, VMEM),
        scratch_shapes=[
            *[pltpu.VMEM(gu, kind) for kind in kinds],
            *[pltpu.VMEM(dn, kind) for kind in kinds],
            pltpu.VMEM((REPS, PAYLOAD, LANES), BF16),
            pltpu.VMEM((9 * LANES, LANES), F32),
            pltpu.VMEM((DN_COLS, RANK), F32),
            pltpu.SemaphoreType.DMA((3 * (GROUPS + 1),)),
        ],
        compiler_params=params(32),
    )(*blocks, *parts, *dn_parts)


MOMENT_GAIN = 0.7 * 0.9 * 0.9
SLOW_GAIN = 0.7 * 1.9


def settled(slow, fast, error, moment):
    combined = slow - fast.astype(F32) + error.astype(F32)
    return slow - MOMENT_GAIN * moment, combined, 0.9 * moment


def shift(value, axis, size, by):
    return lax.ppermute(value, axis, [(i, (i + by) % size) for i in range(size)])


def swap(value):
    return lax.ppermute(value, "core", [(0, 1), (1, 0)])


def exchange(value, axis):
    return lax.all_to_all(value, axis, 0, 0, tiled=False)


def on_device(
    gu_slow, gu_fast, gu_error, gu_moment, gu_basis, dn_slow, dn_fast, dn_error, dn_moment, dn_basis
):
    gu_fast, gu_error = gu_fast[0], gu_error[0]
    dn_fast, dn_error = dn_fast[0], dn_error[0]
    basis = exchange(basis_tiles(gu_basis, dn_basis.T), "z")
    own, oth = lower(gu_slow, gu_fast, gu_error, dn_slow, dn_fast, dn_error)
    came = swap(oth)
    zero, *sends = pair_sums(own, came)
    comes = {by: shift(sends[by - 1], "y", 4, by) for by in (2, 1, 3)}
    rows = list(y_sum(zero, comes))
    for by in (2, 1, 3):
        rows[by] = shift(rows[by], "x", 4, by)
    rows, parts = p_part(rows, basis)
    parts = exchange(parts, ("y", "core", "x"))
    recv = exchange(p_sum(parts, rows), "z")
    a_blocks, q_block = factor(recv)
    payload = pack(exchange(a_blocks, SHARD), q_block)
    mine = {0: payload}
    for by in (2, 1, 3):
        mine[by] = shift(payload, "y", 4, by)
    blocks = [mine[by] for by in range(4)]
    blocks = blocks + [swap(b) for b in blocks]
    gs, ge, gm, ds, de, dm, gb, db = finish(
        blocks,
        settled(gu_slow, gu_fast, gu_error, gu_moment),
        settled(dn_slow, dn_fast, dn_error, dn_moment),
    )
    return gs, ge[None], gm, gb, ds, de[None], dm, db.T


def solution(mesh):
    fine = Mesh(mesh.devices.reshape(4, 2, 8, 4), ("y", "core", "z", "x"))
    rep = ("y", "core")
    weights, shared = P(None, SHARD, None), P(SHARD, None)
    replica = P(rep, None, SHARD, None)
    dn_replica = P(rep, SHARD, None)
    return jax.shard_map(
        on_device,
        mesh=fine,
        in_specs=(
            weights, replica, replica, weights, shared,
            shared, dn_replica, dn_replica, shared, shared,
        ),
        out_specs=(
            weights, replica, weights, shared,
            shared, dn_replica, shared, shared,
        ),
        check_vma=False,
    )
```

```python
import functools

import jax
import jax.numpy as jnp
from jax import lax
from jax.experimental import pallas as pl
from jax.experimental.pallas import tpu as pltpu
from jax.sharding import Mesh
from jax.sharding import PartitionSpec as P

FF = 29568
D = 8192
SHARDS = 32
REPS = 8
GU_COLS = FF // SHARDS
DN_COLS = D // SHARDS
LANES = 128
TILES = FF // LANES
RANK = 64
F32 = jnp.float32
BF16 = jnp.bfloat16
SHARD = ("z", "x")
VMEM = pl.BlockSpec(memory_space=pltpu.VMEM)
HBM = pl.BlockSpec(memory_space=pltpu.HBM)
ANY = pl.BlockSpec(memory_space=pl.ANY)
GROUPS = 4
PER = SHARDS // GROUPS


LIGHT = pl.CostEstimate(flops=1, bytes_accessed=1, transcendentals=0)
HEAVY = pl.CostEstimate(flops=10**13, bytes_accessed=10**11, transcendentals=0)


def params(mib):
    return pltpu.CompilerParams(vmem_limit_bytes=mib * 2**20)


def first_tile(shard):
    return TILES * shard // SHARDS


def offset(shard):
    return GU_COLS * shard - LANES * first_tile(shard)


def has_ninth(shard):
    return offset(shard) > 8 * LANES - GU_COLS


def places():
    return lax.axis_index("y"), lax.axis_index("core"), lax.axis_index("z") * 4 + lax.axis_index("x")


def lane_ids():
    return lax.broadcasted_iota(jnp.int32, (8, LANES), 1)


def group_bounds():
    bounds = [0]
    for g in range(GROUPS):
        bounds.append(min(TILES, first_tile(PER * (g + 1)) + 1) * LANES)
    return bounds


GU_ROWS = SHARDS * 16
DN_TILES = D // REPS // LANES
BLOCK = GU_ROWS + DN_TILES * 8
X_ROWS = 8 * 16 + 16


def lower_kernel(gs, gf, ge, ds, df, de, own, oth, gsv, gfv, gev, dsv, dfv, dev, sems):
    core = lax.axis_index("core")
    bounds = group_bounds()
    copies = []
    for g in range(GROUPS):
        a, n = bounds[g], bounds[g + 1] - bounds[g]
        c, m = DN_COLS * PER * g, DN_COLS * PER
        row = []
        for i, (src, dst) in enumerate(((gs, gsv), (gf, gfv), (ge, gev))):
            at = (slice(None), slice(None), pl.ds(a, n))
            row.append(pltpu.make_async_copy(src.at[at], dst.at[at], sems.at[g, i]))
        for i, (src, dst) in enumerate(((ds, dsv), (df, dfv), (de, dev))):
            at = (slice(None), pl.ds(c, m))
            row.append(pltpu.make_async_copy(src.at[at], dst.at[at], sems.at[g, 3 + i]))
        for copy in row:
            copy.start()
        copies.append(row)
    first = core == 0
    lane = lane_ids()

    def gu_tile(tile):
        at = (slice(None), slice(None), pl.ds(tile * LANES, LANES))
        return gsv[at] - gfv[at].astype(F32) + gev[at].astype(F32)

    def put(yy, x, at, one, two):
        own[4 * yy + x, at : at + 16] = jnp.where(first, one, two).astype(BF16)
        oth[4 * yy + x, at : at + 16] = jnp.where(first, two, one).astype(BF16)

    for shard in range(SHARDS):
        if shard % PER == 0:
            for copy in copies[shard // PER]:
                copy.wait()
        tiles = [gu_tile(first_tile(shard) + j) for j in range(8)]
        if has_ninth(shard):
            tiles[0] = jnp.where(lane[None] < 24, gu_tile(first_tile(shard) + 8), tiles[0])
        for yy in range(4):
            one, two = (tiles[2 * yy + c].reshape(16, LANES) for c in range(2))
            put(yy, shard % 4, 16 * (shard // 4), one, two)
    for x in range(4):
        parts = [[None, None] for _ in range(REPS)]
        for p in range(2):
            sources = []
            for j in range(4):
                at = (slice(None), pl.ds(DN_COLS * (4 * (4 * p + j) + x), DN_COLS))
                sources.append(dsv[at] - dfv[at].astype(F32) + dev[at].astype(F32))
            for r in range(REPS):
                tile = None
                for j in range(4):
                    at = LANES * (r // 4)
                    piece = sources[j][:, at : at + LANES]
                    if j != r % 4:
                        piece = pltpu.roll(piece, 32 * (j - r % 4) % LANES, 1)
                    tile = piece if j == 0 else jnp.where(lane < 32 * j, tile, piece)
                parts[r][p] = tile
        for yy in range(4):
            one, two = (jnp.concatenate(parts[2 * yy + c], axis=0) for c in range(2))
            put(yy, x, 8 * 16, one, two)


def lower(gs, gf, ge, ds, df, de):
    shape = jax.ShapeDtypeStruct((16, X_ROWS, LANES), BF16)
    return pl.pallas_call(
        lower_kernel,
        out_shape=(shape, shape),
        in_specs=[HBM] * 6,
        out_specs=(VMEM, VMEM),
        scratch_shapes=[
            pltpu.VMEM((2, 8, FF), F32),
            pltpu.VMEM((2, 8, FF), BF16),
            pltpu.VMEM((2, 8, FF), BF16),
            pltpu.VMEM((8, D), F32),
            pltpu.VMEM((8, D), BF16),
            pltpu.VMEM((8, D), BF16),
            pltpu.SemaphoreType.DMA((GROUPS, 6)),
        ],
        compiler_params=params(54),
        cost_estimate=LIGHT,
    )(gs, gf, ge, ds, df, de)


B_ROWS = LANES + 16


def basis_kernel(gu_any, dn_any, out, rows, dn_rows, gu, dn_t, sems):
    y, core, shard = places()
    rep = 2 * y + core
    start = LANES - offset(shard)
    copies = [
        pltpu.make_async_copy(gu_any, gu, sems.at[0]),
        pltpu.make_async_copy(dn_any, dn_t, sems.at[1]),
    ]
    for copy in copies:
        copy.start()
    for copy in copies:
        copy.wait()
    rows[0:LANES, :] = jnp.zeros((LANES, LANES), F32)
    rows[LANES : LANES + GU_COLS, :] = gu[...].astype(F32)
    rows[LANES + GU_COLS :, :] = jnp.zeros((rows.shape[0] - LANES - GU_COLS, LANES), F32)
    tile = rows[pl.ds(start + LANES * rep, LANES), :]
    ninth = rows[pl.ds(start + LANES * 8, LANES), :]
    tile = tile + jnp.where(rep == 0, ninth, 0.0)
    dn_rows[...] = dn_t[...].astype(F32).T
    dn = dn_rows[pl.ds(pl.multiple_of(32 * rep, 32), 32), :]
    dn = jnp.concatenate([dn[0:16], dn[16:32]], axis=1)
    block = jnp.concatenate([tile, dn], axis=0).astype(BF16)
    for z in range(8):
        out[z] = block


def basis_tiles(gu, dn_t):
    return pl.pallas_call(
        basis_kernel,
        out_shape=jax.ShapeDtypeStruct((8, B_ROWS, LANES), BF16),
        in_specs=[HBM, HBM],
        out_specs=VMEM,
        scratch_shapes=[
            pltpu.VMEM((1280, LANES), F32),
            pltpu.VMEM((DN_COLS, RANK), F32),
            pltpu.VMEM((GU_COLS, LANES), BF16),
            pltpu.VMEM((RANK, DN_COLS), BF16),
            pltpu.SemaphoreType.DMA((2,)),
        ],
        compiler_params=params(16),
    )(gu, dn_t)


def pair_kernel(own, came, after, zero, one, two, three):
    y = lax.axis_index("y")
    for k, out in ((2, two), (1, one), (3, three), (0, zero)):
        to = 4 * lax.rem(y + k, 4)
        for x in range(4):
            total = own[to + x].astype(F32) + came[to + x].astype(F32)
            out[x] = total.astype(out.dtype)


def pair_sums(own, came, after):
    block = (4, X_ROWS, LANES)
    return pl.pallas_call(
        pair_kernel,
        out_shape=(
            jax.ShapeDtypeStruct(block, F32),
            *[jax.ShapeDtypeStruct(block, BF16)] * 3,
        ),
        in_specs=[VMEM] * 2 + [ANY],
        out_specs=(VMEM,) * 4,
        compiler_params=params(16),
        cost_estimate=LIGHT,
    )(own, came, after)


def y_sum_kernel(zero, one, two, three, x0, x1, x2, x3, sums):
    for x in range(4):
        total = zero[x]
        for ref in (one, two, three):
            total = total + ref[x].astype(F32)
        sums[x] = total.astype(BF16)
    x = lax.axis_index("x")
    for k, ref in enumerate((x0, x1, x2, x3)):
        ref[...] = sums[lax.rem(x + k, 4)]


def y_sum(zero, comes):
    return pl.pallas_call(
        y_sum_kernel,
        out_shape=(jax.ShapeDtypeStruct((X_ROWS, LANES), BF16),) * 4,
        in_specs=[VMEM] * 4,
        out_specs=(VMEM,) * 4,
        scratch_shapes=[pltpu.VMEM((4, X_ROWS, LANES), BF16)],
        compiler_params=params(16),
        cost_estimate=HEAVY,
    )(zero, comes[1], comes[2], comes[3])


P_ROWS = 48
Z_ROWS = 4 * 24 + P_ROWS


def p_part_kernel(l0, l1, l2, l3, basis, rows, out, stage):
    x = lax.axis_index("x")
    for k, ref in enumerate((l0, l1, l2, l3)):
        stage[lax.rem(x - k + 4, 4)] = ref[...]
    lows = [stage[x] for x in range(4)]
    sums = [stage[x, 8 * 16 : X_ROWS, :].astype(F32) for x in range(4)]
    gu = jnp.zeros((64, LANES), F32)
    for z in range(0, 8, 2):
        left = [
            jnp.concatenate([low[16 * i : 16 * i + 16] for low in lows], axis=0)
            for i in (z, z + 1)
        ]
        rows[z, 0:64, :] = left[0]
        rows[z + 1, 0:64, :] = left[1]
        right = basis[z : z + 2, 0:LANES, :].reshape(2 * LANES, LANES)
        gu = gu + jnp.dot(jnp.concatenate(left, axis=1), right, preferred_element_type=F32)
    dn = jnp.zeros((32, RANK), F32)
    for p in range(2):
        left = [total[8 * p : 8 * p + 8] for total in sums]
        left = jnp.concatenate(left, axis=0).astype(BF16)
        for z in range(4 * p, 4 * p + 4):
            rows[z, 64:96, :] = left
        right = basis[4 * p : 4 * p + 4, LANES:B_ROWS, :].astype(F32)
        right = jnp.concatenate([right[:, :, 0:RANK], right[:, :, RANK:LANES]], axis=1)
        right = right.reshape(LANES, RANK).astype(BF16)
        dn = dn + jnp.dot(left, right, preferred_element_type=F32)
    parts = [
        jnp.concatenate(
            [
                gu[16 * x : 16 * x + 8, 0:RANK],
                gu[16 * x + 8 : 16 * x + 16, RANK:LANES],
                dn[8 * x : 8 * x + 8],
            ],
            axis=0,
        )
        for x in range(4)
    ]
    block = jnp.concatenate(
        [jnp.concatenate(parts[k : k + 2], axis=1) for k in (0, 2)], axis=0
    ).astype(BF16)
    for member in range(32):
        out[member] = block


def p_part(rows, basis):
    return pl.pallas_call(
        p_part_kernel,
        out_shape=(
            jax.ShapeDtypeStruct((8, 96, LANES), BF16),
            jax.ShapeDtypeStruct((32, P_ROWS, LANES), BF16),
        ),
        in_specs=[VMEM] * 5,
        out_specs=(VMEM,) * 2,
        scratch_shapes=[pltpu.VMEM((4, X_ROWS, LANES), BF16)],
        compiler_params=params(16),
    )(*rows, basis)


def p_sum_kernel(ps, rows, out):
    total = jnp.sum(ps[...].astype(F32), axis=0).astype(BF16)
    for z in range(8):
        out[z, 0:96, :] = rows[z]
        out[z, 96:Z_ROWS, :] = total


def p_sum(ps, rows):
    return pl.pallas_call(
        p_sum_kernel,
        out_shape=jax.ShapeDtypeStruct((8, Z_ROWS, LANES), BF16),
        in_specs=[VMEM, VMEM],
        out_specs=VMEM,
        compiler_params=params(16),
    )(ps, rows)


def inverse_factors(grams):
    eye = (
        lax.broadcasted_iota(jnp.int32, (RANK, RANK), 0)
        == lax.broadcasted_iota(jnp.int32, (RANK, RANK), 1)
    ).astype(F32)
    sub = lax.broadcasted_iota(jnp.int32, (8, LANES), 0)

    def spread_lane(x, k):
        return jnp.broadcast_to(x[:, k : k + 1], (8, LANES))

    def spread_row(x, k):
        return jnp.broadcast_to(x[k : k + 1], (8, LANES))

    works = []
    for gram in grams:
        work = jnp.concatenate([gram, eye], axis=1)
        works.append([work[8 * b : 8 * b + 8] for b in range(8)])
    outs = [[] for _ in grams]
    for now in range(8):
        pivots = [jnp.ones((8, LANES), F32) for _ in grams]
        ratios, rows = [[] for _ in grams], [[] for _ in grams]
        spread = [[spread_lane(work[now], 8 * now + j) for j in range(8)] for work in works]
        for j in range(8):
            for m, work in enumerate(works):
                cols = spread[m]
                pivot = spread_row(cols[j], j)
                inverse = 1.0 / pivot
                pivots[m] = jnp.where(sub == j, pivot, pivots[m])
                rows[m].append(spread_row(work[now], j) * inverse)
                ratios[m].append([spread_row(cols[i], j) * inverse for i in range(j + 1, 8)])
                if j < 7:
                    below = jnp.where(sub > j, cols[j], 0.0)
                    for i in range(j + 1, 8):
                        cols[i] = cols[i] - below * ratios[m][j][i - j - 1]
                    work[now] = work[now] - below * rows[m][j]
        for m, work in enumerate(works):
            for b in range(now + 1, 8):
                cols = [spread_lane(work[b], 8 * now + j) for j in range(8)]
                for j in range(8):
                    for i in range(j + 1, 8):
                        cols[i] = cols[i] - cols[j] * ratios[m][j][i - j - 1]
                    work[b] = work[b] - cols[j] * rows[m][j]
            outs[m].append(work[now] * lax.rsqrt(pivots[m]))
    return [jnp.concatenate(out, axis=0)[:, RANK:LANES] for out in outs]


def exact_dot(a, b, dims):
    return lax.dot_general(
        a, b, (dims, ((), ())), precision=lax.Precision.HIGHEST, preferred_element_type=F32
    )


def factor_kernel(recv, a_out, q_out, q_rows):
    block = recv[...].astype(F32)
    gu = block[:, 0:64, :].reshape(8, 4, 16, LANES)
    columns = [gu[:, :, 0:8], gu[:, :, 8:16], block[:, 64:96, :]]
    columns = [column.reshape(256, LANES).astype(BF16) for column in columns]
    lefts = []
    for m in range(3):
        left = [
            block[:, at : at + 8, RANK * b : RANK * b + RANK]
            for at in (96 + 8 * m, 120 + 8 * m)
            for b in range(2)
        ]
        lefts.append(jnp.stack(left, axis=1).reshape(256, RANK))
    grams = [exact_dot(p, p, ((0,), (0,))) for p in lefts]
    inverses = inverse_factors(grams)
    hs = [exact_dot(p, v, ((1,), (1,))).astype(BF16) for p, v in zip(lefts, inverses)]
    recons, qs = [], []
    for h, column in zip(hs, columns):
        q = lax.dot_general(column, h, (((0,), (0,)), ((), ())), preferred_element_type=F32)
        q = (q * (1.0 / REPS)).astype(BF16)
        qs.append(q.astype(F32))
        recon = lax.dot_general(h, q, (((1,), (1,)), ((), ())), preferred_element_type=F32)
        recons.append(recon.reshape(SHARDS, 8, LANES))
    a_out[...] = jnp.concatenate(recons, axis=1).astype(BF16)
    q_rows[...] = qs[2]
    dn = q_rows[pl.ds(pl.multiple_of(32 * lax.rem(lax.axis_index("z"), 4), 32), 32), :]
    dn = jnp.concatenate([dn, jnp.zeros_like(dn)], axis=1)
    gu = jnp.concatenate(qs[:2], axis=1)
    q_out[...] = jnp.concatenate([gu, dn], axis=0).astype(BF16)


def factor(recv):
    return pl.pallas_call(
        factor_kernel,
        out_shape=(
            jax.ShapeDtypeStruct((SHARDS, 24, LANES), BF16),
            jax.ShapeDtypeStruct((Q_ROWS, LANES), BF16),
        ),
        in_specs=[VMEM],
        out_specs=(VMEM, VMEM),
        scratch_shapes=[pltpu.VMEM((LANES, RANK), F32)],
        compiler_params=params(32),
    )(recv)


Q_ROWS = LANES + 32
PAYLOAD = BLOCK + Q_ROWS


def pack_kernel(rows, q, out):
    for s in range(SHARDS):
        out[16 * s : 16 * s + 16, :] = rows[s].astype(F32)[0:16].astype(BF16)
    for x in range(4):
        two = [rows[16 * p + x].astype(F32)[16:24] for p in range(2)]
        at = GU_ROWS + 16 * x
        out[at : at + 16, :] = jnp.concatenate(two, axis=0).astype(BF16)
    out[BLOCK:PAYLOAD, :] = q[...]


def pack(rows, q):
    return pl.pallas_call(
        pack_kernel,
        out_shape=jax.ShapeDtypeStruct((PAYLOAD, LANES), BF16),
        in_specs=[VMEM, VMEM],
        out_specs=VMEM,
        compiler_params=params(16),
    )(rows, q)


def finish_kernel(
    b0, b1, b2, b3, b4, b5, b6, b7, gs, gc, gm, ds, dc, dm,
    gs_o, ge_o, gm_o, ds_o, de_o, dm_o, gb_o, db_o,
    gs_v, ge_v, gm_v, ds_v, de_v, dm_v, stage, q_full, q_dn, sems,
):
    bounds = [first_tile(PER * g) * LANES for g in range(GROUPS + 1)]
    y, core, mine = places()
    for i, block in enumerate((b0, b1, b2, b3, b4, b5, b6, b7)):
        rep = 2 * lax.rem(y - i % 4 + 4, 4) + (core if i < 4 else 1 - core)
        stage[rep] = block[...]

    copies = []

    def send(pairs, at):
        for src, dst in pairs:
            copies.append(pltpu.make_async_copy(src.at[at], dst.at[at], sems.at[len(copies)]))
            copies[-1].start()

    lane = lane_ids()

    def gu_recon(rep, shard):
        return stage[rep, 16 * shard : 16 * shard + 16, :].astype(F32).reshape(2, 8, LANES)

    for g in range(GROUPS):
        for shard in range(PER * g, PER * (g + 1)):
            for j in range(first_tile(shard + 1) - first_tile(shard)):
                recon = gu_recon(j, shard)
                if j == 0 and offset(shard) > 0:
                    other = gu_recon(0 if has_ninth(shard - 1) else 7, shard - 1)
                    recon = jnp.where(lane[None] < offset(shard), other, recon)
                at = (slice(None), slice(None), pl.ds((first_tile(shard) + j) * LANES, LANES))
                gs_v[at] = gs[at] - SLOW_GAIN * recon
                ge_v[at] = (gc[at] - recon).astype(BF16)
                gm_v[at] = gm[at] + recon
        send(
            ((gs_v, gs_o), (ge_v, ge_o), (gm_v, gm_o)),
            (slice(None), slice(None), pl.ds(bounds[g], bounds[g + 1] - bounds[g])),
        )
    tiles = [stage[r, GU_ROWS:BLOCK, :].astype(F32) for r in range(REPS)]
    for shard in range(SHARDS):
        z, x = shard // 4, shard % 4
        q, a = 2 * x + z // 4, z % 4
        for half in range(2):
            recon = None
            for k in range(4):
                piece = tiles[4 * half + k][8 * q : 8 * q + 8]
                if k != a:
                    piece = pltpu.roll(piece, 32 * (k - a) % LANES, 1)
                recon = piece if k == 0 else jnp.where(lane < 32 * k, recon, piece)
            at = (slice(None), pl.ds(DN_COLS * shard + LANES * half, LANES))
            ds_v[at] = ds[at] - SLOW_GAIN * recon
            de_v[at] = (dc[at] - recon).astype(BF16)
            dm_v[at] = dm[at] + recon
    send(((ds_v, ds_o), (de_v, de_o), (dm_v, dm_o)), (slice(None), slice(None)))

    for r in range(REPS):
        block = stage[r, BLOCK:PAYLOAD, :].astype(F32)
        q_full[LANES * r : LANES * r + LANES, :] = block[0:LANES]
        if r == 0:
            q_full[8 * LANES : 9 * LANES, :] = block[0:LANES]
        q_dn[32 * r : 32 * r + 32, :] = block[LANES:Q_ROWS, 0:RANK]
    gb_o[...] = q_full[pl.ds(offset(mine), GU_COLS), :].astype(BF16)
    db_o[...] = q_dn[...].T.astype(BF16)
    for copy in copies:
        copy.wait()


def finish(blocks, parts, dn_parts):
    gu, dn = (2, 8, FF), (8, D)
    kinds = (F32, BF16, F32)
    return pl.pallas_call(
        finish_kernel,
        out_shape=(
            *[jax.ShapeDtypeStruct(gu, kind) for kind in kinds],
            *[jax.ShapeDtypeStruct(dn, kind) for kind in kinds],
            jax.ShapeDtypeStruct((GU_COLS, LANES), BF16),
            jax.ShapeDtypeStruct((RANK, DN_COLS), BF16),
        ),
        in_specs=[VMEM] * 14,
        out_specs=(ANY,) * 6 + (VMEM, VMEM),
        scratch_shapes=[
            *[pltpu.VMEM(gu, kind) for kind in kinds],
            *[pltpu.VMEM(dn, kind) for kind in kinds],
            pltpu.VMEM((REPS, PAYLOAD, LANES), BF16),
            pltpu.VMEM((9 * LANES, LANES), F32),
            pltpu.VMEM((DN_COLS, RANK), F32),
            pltpu.SemaphoreType.DMA((3 * (GROUPS + 1),)),
        ],
        compiler_params=params(32),
    )(*blocks, *parts, *dn_parts)


MOMENT_GAIN = 0.7 * 0.9 * 0.9
SLOW_GAIN = 0.7 * 1.9


def settled(slow, fast, error, moment):
    combined = slow - fast.astype(F32) + error.astype(F32)
    return slow - MOMENT_GAIN * moment, combined, 0.9 * moment


def shift(value, axis, size, by):
    return lax.ppermute(value, axis, [(i, (i + by) % size) for i in range(size)])


def swap(value):
    return lax.ppermute(value, "core", [(0, 1), (1, 0)])


def exchange(value, axis):
    return lax.all_to_all(value, axis, 0, 0, tiled=False)


def on_device(
    gu_slow, gu_fast, gu_error, gu_moment, gu_basis, dn_slow, dn_fast, dn_error, dn_moment, dn_basis
):
    gu_fast, gu_error = gu_fast[0], gu_error[0]
    dn_fast, dn_error = dn_fast[0], dn_error[0]
    tiles = basis_tiles(gu_basis, dn_basis.T)
    basis = exchange(tiles, "z")
    own, oth = lower(gu_slow, gu_fast, gu_error, dn_slow, dn_fast, dn_error)
    came = swap(oth)
    zero, *sends = pair_sums(own, came, tiles)
    comes = {by: shift(sends[by - 1], "y", 4, by) for by in (2, 1, 3)}
    rows = list(y_sum(zero, comes))
    for by in (2, 1, 3):
        rows[by] = shift(rows[by], "x", 4, by)
    rows, parts = p_part(rows, basis)
    parts = exchange(parts, ("y", "core", "x"))
    recv = exchange(p_sum(parts, rows), "z")
    a_blocks, q_block = factor(recv)
    payload = pack(exchange(a_blocks, SHARD), q_block)
    mine = {0: payload}
    for by in (2, 1, 3):
        mine[by] = shift(payload, "y", 4, by)
    blocks = [mine[by] for by in range(4)]
    blocks = blocks + [swap(b) for b in blocks]
    gs, ge, gm, ds, de, dm, gb, db = finish(
        blocks,
        settled(gu_slow, gu_fast, gu_error, gu_moment),
        settled(dn_slow, dn_fast, dn_error, dn_moment),
    )
    return gs, ge[None], gm, gb, ds, de[None], dm, db.T


def solution(mesh):
    fine = Mesh(mesh.devices.reshape(4, 2, 8, 4), ("y", "core", "z", "x"))
    rep = ("y", "core")
    weights, shared = P(None, SHARD, None), P(SHARD, None)
    replica = P(rep, None, SHARD, None)
    dn_replica = P(rep, SHARD, None)
    return jax.shard_map(
        on_device,
        mesh=fine,
        in_specs=(
            weights, replica, replica, weights, shared,
            shared, dn_replica, dn_replica, shared, shared,
        ),
        out_specs=(
            weights, replica, weights, shared,
            shared, dn_replica, shared, shared,
        ),
        check_vma=False,
    )
```

```python
import functools

import jax
import jax.numpy as jnp
from jax import lax
from jax.experimental import pallas as pl
from jax.experimental.pallas import tpu as pltpu
from jax.sharding import Mesh
from jax.sharding import PartitionSpec as P

FF = 29568
D = 8192
SHARDS = 32
REPS = 8
GU_COLS = FF // SHARDS
DN_COLS = D // SHARDS
LANES = 128
TILES = FF // LANES
RANK = 64
F32 = jnp.float32
BF16 = jnp.bfloat16
SHARD = ("z", "x")
VMEM = pl.BlockSpec(memory_space=pltpu.VMEM)
HBM = pl.BlockSpec(memory_space=pltpu.HBM)
ANY = pl.BlockSpec(memory_space=pl.ANY)
GROUPS = 4
PER = SHARDS // GROUPS


LIGHT = pl.CostEstimate(flops=1, bytes_accessed=1, transcendentals=0)
HEAVY = pl.CostEstimate(flops=3 * 10**10, bytes_accessed=10**8, transcendentals=0)


def params(mib):
    return pltpu.CompilerParams(vmem_limit_bytes=mib * 2**20)


def first_tile(shard):
    return TILES * shard // SHARDS


def offset(shard):
    return GU_COLS * shard - LANES * first_tile(shard)


def has_ninth(shard):
    return offset(shard) > 8 * LANES - GU_COLS


def places():
    return lax.axis_index("y"), lax.axis_index("core"), lax.axis_index("z") * 4 + lax.axis_index("x")


def lane_ids():
    return lax.broadcasted_iota(jnp.int32, (8, LANES), 1)


def group_bounds():
    bounds = [0]
    for g in range(GROUPS):
        bounds.append(min(TILES, first_tile(PER * (g + 1)) + 1) * LANES)
    return bounds


GU_ROWS = SHARDS * 16
DN_TILES = D // REPS // LANES
BLOCK = GU_ROWS + DN_TILES * 8
X_ROWS = 8 * 16 + 16


def lower_kernel(gs, gf, ge, ds, df, de, own, oth, gsv, gfv, gev, dsv, dfv, dev, sems):
    core = lax.axis_index("core")
    bounds = group_bounds()
    copies = []
    for g in range(GROUPS):
        a, n = bounds[g], bounds[g + 1] - bounds[g]
        c, m = DN_COLS * PER * g, DN_COLS * PER
        row = []
        for i, (src, dst) in enumerate(((gs, gsv), (gf, gfv), (ge, gev))):
            at = (slice(None), slice(None), pl.ds(a, n))
            row.append(pltpu.make_async_copy(src.at[at], dst.at[at], sems.at[g, i]))
        for i, (src, dst) in enumerate(((ds, dsv), (df, dfv), (de, dev))):
            at = (slice(None), pl.ds(c, m))
            row.append(pltpu.make_async_copy(src.at[at], dst.at[at], sems.at[g, 3 + i]))
        for copy in row:
            copy.start()
        copies.append(row)
    first = core == 0
    lane = lane_ids()

    def gu_tile(tile):
        at = (slice(None), slice(None), pl.ds(tile * LANES, LANES))
        return gsv[at] - gfv[at].astype(F32) + gev[at].astype(F32)

    def put(yy, x, at, one, two):
        own[4 * yy + x, at : at + 16] = jnp.where(first, one, two).astype(BF16)
        oth[4 * yy + x, at : at + 16] = jnp.where(first, two, one).astype(BF16)

    for shard in range(SHARDS):
        if shard % PER == 0:
            for copy in copies[shard // PER]:
                copy.wait()
        tiles = [gu_tile(first_tile(shard) + j) for j in range(8)]
        if has_ninth(shard):
            tiles[0] = jnp.where(lane[None] < 24, gu_tile(first_tile(shard) + 8), tiles[0])
        for yy in range(4):
            one, two = (tiles[2 * yy + c].reshape(16, LANES) for c in range(2))
            put(yy, shard % 4, 16 * (shard // 4), one, two)
    for x in range(4):
        parts = [[None, None] for _ in range(REPS)]
        for p in range(2):
            sources = []
            for j in range(4):
                at = (slice(None), pl.ds(DN_COLS * (4 * (4 * p + j) + x), DN_COLS))
                sources.append(dsv[at] - dfv[at].astype(F32) + dev[at].astype(F32))
            for r in range(REPS):
                tile = None
                for j in range(4):
                    at = LANES * (r // 4)
                    piece = sources[j][:, at : at + LANES]
                    if j != r % 4:
                        piece = pltpu.roll(piece, 32 * (j - r % 4) % LANES, 1)
                    tile = piece if j == 0 else jnp.where(lane < 32 * j, tile, piece)
                parts[r][p] = tile
        for yy in range(4):
            one, two = (jnp.concatenate(parts[2 * yy + c], axis=0) for c in range(2))
            put(yy, x, 8 * 16, one, two)


def lower(gs, gf, ge, ds, df, de):
    shape = jax.ShapeDtypeStruct((16, X_ROWS, LANES), BF16)
    return pl.pallas_call(
        lower_kernel,
        out_shape=(shape, shape),
        in_specs=[HBM] * 6,
        out_specs=(VMEM, VMEM),
        scratch_shapes=[
            pltpu.VMEM((2, 8, FF), F32),
            pltpu.VMEM((2, 8, FF), BF16),
            pltpu.VMEM((2, 8, FF), BF16),
            pltpu.VMEM((8, D), F32),
            pltpu.VMEM((8, D), BF16),
            pltpu.VMEM((8, D), BF16),
            pltpu.SemaphoreType.DMA((GROUPS, 6)),
        ],
        compiler_params=params(54),
        cost_estimate=LIGHT,
    )(gs, gf, ge, ds, df, de)


B_ROWS = LANES + 16


def basis_kernel(gu_any, dn_any, out, rows, dn_rows, gu, dn_t, sems):
    y, core, shard = places()
    rep = 2 * y + core
    start = LANES - offset(shard)
    copies = [
        pltpu.make_async_copy(gu_any, gu, sems.at[0]),
        pltpu.make_async_copy(dn_any, dn_t, sems.at[1]),
    ]
    for copy in copies:
        copy.start()
    for copy in copies:
        copy.wait()
    rows[0:LANES, :] = jnp.zeros((LANES, LANES), F32)
    rows[LANES : LANES + GU_COLS, :] = gu[...].astype(F32)
    rows[LANES + GU_COLS :, :] = jnp.zeros((rows.shape[0] - LANES - GU_COLS, LANES), F32)
    tile = rows[pl.ds(start + LANES * rep, LANES), :]
    ninth = rows[pl.ds(start + LANES * 8, LANES), :]
    tile = tile + jnp.where(rep == 0, ninth, 0.0)
    dn_rows[...] = dn_t[...].astype(F32).T
    dn = dn_rows[pl.ds(pl.multiple_of(32 * rep, 32), 32), :]
    dn = jnp.concatenate([dn[0:16], dn[16:32]], axis=1)
    block = jnp.concatenate([tile, dn], axis=0).astype(BF16)
    for z in range(8):
        out[z] = block


def basis_tiles(gu, dn_t):
    return pl.pallas_call(
        basis_kernel,
        out_shape=jax.ShapeDtypeStruct((8, B_ROWS, LANES), BF16),
        in_specs=[HBM, HBM],
        out_specs=VMEM,
        scratch_shapes=[
            pltpu.VMEM((1280, LANES), F32),
            pltpu.VMEM((DN_COLS, RANK), F32),
            pltpu.VMEM((GU_COLS, LANES), BF16),
            pltpu.VMEM((RANK, DN_COLS), BF16),
            pltpu.SemaphoreType.DMA((2,)),
        ],
        compiler_params=params(16),
    )(gu, dn_t)


def pair_kernel(own, came, after, zero, one, two, three):
    y = lax.axis_index("y")
    for k, out in ((2, two), (1, one), (3, three), (0, zero)):
        to = 4 * lax.rem(y + k, 4)
        for x in range(4):
            total = own[to + x].astype(F32) + came[to + x].astype(F32)
            out[x] = total.astype(out.dtype)


def pair_sums(own, came, after):
    block = (4, X_ROWS, LANES)
    return pl.pallas_call(
        pair_kernel,
        out_shape=(
            jax.ShapeDtypeStruct(block, F32),
            *[jax.ShapeDtypeStruct(block, BF16)] * 3,
        ),
        in_specs=[VMEM] * 2 + [ANY],
        out_specs=(VMEM,) * 4,
        compiler_params=params(16),
        cost_estimate=LIGHT,
    )(own, came, after)


def y_sum_kernel(zero, one, two, three, x0, x1, x2, x3, sums):
    for x in range(4):
        total = zero[x]
        for ref in (one, two, three):
            total = total + ref[x].astype(F32)
        sums[x] = total.astype(BF16)
    x = lax.axis_index("x")
    for k, ref in enumerate((x0, x1, x2, x3)):
        ref[...] = sums[lax.rem(x + k, 4)]


def y_sum(zero, comes):
    return pl.pallas_call(
        y_sum_kernel,
        out_shape=(jax.ShapeDtypeStruct((X_ROWS, LANES), BF16),) * 4,
        in_specs=[VMEM] * 4,
        out_specs=(VMEM,) * 4,
        scratch_shapes=[pltpu.VMEM((4, X_ROWS, LANES), BF16)],
        compiler_params=params(16),
        cost_estimate=HEAVY,
    )(zero, comes[1], comes[2], comes[3])


P_ROWS = 48
Z_ROWS = 4 * 24 + P_ROWS


def p_part_kernel(l0, l1, l2, l3, basis, rows, out, stage):
    x = lax.axis_index("x")
    for k, ref in enumerate((l0, l1, l2, l3)):
        stage[lax.rem(x - k + 4, 4)] = ref[...]
    lows = [stage[x] for x in range(4)]
    sums = [stage[x, 8 * 16 : X_ROWS, :].astype(F32) for x in range(4)]
    gu = jnp.zeros((64, LANES), F32)
    for z in range(0, 8, 2):
        left = [
            jnp.concatenate([low[16 * i : 16 * i + 16] for low in lows], axis=0)
            for i in (z, z + 1)
        ]
        rows[z, 0:64, :] = left[0]
        rows[z + 1, 0:64, :] = left[1]
        right = basis[z : z + 2, 0:LANES, :].reshape(2 * LANES, LANES)
        gu = gu + jnp.dot(jnp.concatenate(left, axis=1), right, preferred_element_type=F32)
    dn = jnp.zeros((32, RANK), F32)
    for p in range(2):
        left = [total[8 * p : 8 * p + 8] for total in sums]
        left = jnp.concatenate(left, axis=0).astype(BF16)
        for z in range(4 * p, 4 * p + 4):
            rows[z, 64:96, :] = left
        right = basis[4 * p : 4 * p + 4, LANES:B_ROWS, :].astype(F32)
        right = jnp.concatenate([right[:, :, 0:RANK], right[:, :, RANK:LANES]], axis=1)
        right = right.reshape(LANES, RANK).astype(BF16)
        dn = dn + jnp.dot(left, right, preferred_element_type=F32)
    parts = [
        jnp.concatenate(
            [
                gu[16 * x : 16 * x + 8, 0:RANK],
                gu[16 * x + 8 : 16 * x + 16, RANK:LANES],
                dn[8 * x : 8 * x + 8],
            ],
            axis=0,
        )
        for x in range(4)
    ]
    block = jnp.concatenate(
        [jnp.concatenate(parts[k : k + 2], axis=1) for k in (0, 2)], axis=0
    ).astype(BF16)
    for member in range(32):
        out[member] = block


def p_part(rows, basis):
    return pl.pallas_call(
        p_part_kernel,
        out_shape=(
            jax.ShapeDtypeStruct((8, 96, LANES), BF16),
            jax.ShapeDtypeStruct((32, P_ROWS, LANES), BF16),
        ),
        in_specs=[VMEM] * 5,
        out_specs=(VMEM,) * 2,
        scratch_shapes=[pltpu.VMEM((4, X_ROWS, LANES), BF16)],
        compiler_params=params(16),
    )(*rows, basis)


def p_sum_kernel(ps, rows, out):
    total = jnp.sum(ps[...].astype(F32), axis=0).astype(BF16)
    for z in range(8):
        out[z, 0:96, :] = rows[z]
        out[z, 96:Z_ROWS, :] = total


def p_sum(ps, rows):
    return pl.pallas_call(
        p_sum_kernel,
        out_shape=jax.ShapeDtypeStruct((8, Z_ROWS, LANES), BF16),
        in_specs=[VMEM, VMEM],
        out_specs=VMEM,
        compiler_params=params(16),
    )(ps, rows)


def inverse_factors(grams):
    eye = (
        lax.broadcasted_iota(jnp.int32, (RANK, RANK), 0)
        == lax.broadcasted_iota(jnp.int32, (RANK, RANK), 1)
    ).astype(F32)
    sub = lax.broadcasted_iota(jnp.int32, (8, LANES), 0)

    def spread_lane(x, k):
        return jnp.broadcast_to(x[:, k : k + 1], (8, LANES))

    def spread_row(x, k):
        return jnp.broadcast_to(x[k : k + 1], (8, LANES))

    works = []
    for gram in grams:
        work = jnp.concatenate([gram, eye], axis=1)
        works.append([work[8 * b : 8 * b + 8] for b in range(8)])
    outs = [[] for _ in grams]
    for now in range(8):
        pivots = [jnp.ones((8, LANES), F32) for _ in grams]
        ratios, rows = [[] for _ in grams], [[] for _ in grams]
        spread = [[spread_lane(work[now], 8 * now + j) for j in range(8)] for work in works]
        for j in range(8):
            for m, work in enumerate(works):
                cols = spread[m]
                pivot = spread_row(cols[j], j)
                inverse = 1.0 / pivot
                pivots[m] = jnp.where(sub == j, pivot, pivots[m])
                rows[m].append(spread_row(work[now], j) * inverse)
                ratios[m].append([spread_row(cols[i], j) * inverse for i in range(j + 1, 8)])
                if j < 7:
                    below = jnp.where(sub > j, cols[j], 0.0)
                    for i in range(j + 1, 8):
                        cols[i] = cols[i] - below * ratios[m][j][i - j - 1]
                    work[now] = work[now] - below * rows[m][j]
        for m, work in enumerate(works):
            for b in range(now + 1, 8):
                cols = [spread_lane(work[b], 8 * now + j) for j in range(8)]
                for j in range(8):
                    for i in range(j + 1, 8):
                        cols[i] = cols[i] - cols[j] * ratios[m][j][i - j - 1]
                    work[b] = work[b] - cols[j] * rows[m][j]
            outs[m].append(work[now] * lax.rsqrt(pivots[m]))
    return [jnp.concatenate(out, axis=0)[:, RANK:LANES] for out in outs]


def exact_dot(a, b, dims):
    return lax.dot_general(
        a, b, (dims, ((), ())), precision=lax.Precision.HIGHEST, preferred_element_type=F32
    )


def factor_kernel(recv, a_out, q_out, q_rows):
    block = recv[...].astype(F32)
    gu = block[:, 0:64, :].reshape(8, 4, 16, LANES)
    columns = [gu[:, :, 0:8], gu[:, :, 8:16], block[:, 64:96, :]]
    columns = [column.reshape(256, LANES).astype(BF16) for column in columns]
    lefts = []
    for m in range(3):
        left = [
            block[:, at : at + 8, RANK * b : RANK * b + RANK]
            for at in (96 + 8 * m, 120 + 8 * m)
            for b in range(2)
        ]
        lefts.append(jnp.stack(left, axis=1).reshape(256, RANK))
    grams = [exact_dot(p, p, ((0,), (0,))) for p in lefts]
    inverses = inverse_factors(grams)
    hs = [exact_dot(p, v, ((1,), (1,))).astype(BF16) for p, v in zip(lefts, inverses)]
    recons, qs = [], []
    for h, column in zip(hs, columns):
        q = lax.dot_general(column, h, (((0,), (0,)), ((), ())), preferred_element_type=F32)
        q = (q * (1.0 / REPS)).astype(BF16)
        qs.append(q.astype(F32))
        recon = lax.dot_general(h, q, (((1,), (1,)), ((), ())), preferred_element_type=F32)
        recons.append(recon.reshape(SHARDS, 8, LANES))
    a_out[...] = jnp.concatenate(recons, axis=1).astype(BF16)
    q_rows[...] = qs[2]
    dn = q_rows[pl.ds(pl.multiple_of(32 * lax.rem(lax.axis_index("z"), 4), 32), 32), :]
    dn = jnp.concatenate([dn, jnp.zeros_like(dn)], axis=1)
    gu = jnp.concatenate(qs[:2], axis=1)
    q_out[...] = jnp.concatenate([gu, dn], axis=0).astype(BF16)


def factor(recv):
    return pl.pallas_call(
        factor_kernel,
        out_shape=(
            jax.ShapeDtypeStruct((SHARDS, 24, LANES), BF16),
            jax.ShapeDtypeStruct((Q_ROWS, LANES), BF16),
        ),
        in_specs=[VMEM],
        out_specs=(VMEM, VMEM),
        scratch_shapes=[pltpu.VMEM((LANES, RANK), F32)],
        compiler_params=params(32),
    )(recv)


Q_ROWS = LANES + 32
PAYLOAD = BLOCK + Q_ROWS


def pack_kernel(rows, q, out):
    for s in range(SHARDS):
        out[16 * s : 16 * s + 16, :] = rows[s].astype(F32)[0:16].astype(BF16)
    for x in range(4):
        two = [rows[16 * p + x].astype(F32)[16:24] for p in range(2)]
        at = GU_ROWS + 16 * x
        out[at : at + 16, :] = jnp.concatenate(two, axis=0).astype(BF16)
    out[BLOCK:PAYLOAD, :] = q[...]


def pack(rows, q):
    return pl.pallas_call(
        pack_kernel,
        out_shape=jax.ShapeDtypeStruct((PAYLOAD, LANES), BF16),
        in_specs=[VMEM, VMEM],
        out_specs=VMEM,
        compiler_params=params(16),
    )(rows, q)


def finish_kernel(
    b0, b1, b2, b3, b4, b5, b6, b7, gs, gc, gm, ds, dc, dm,
    gs_o, ge_o, gm_o, ds_o, de_o, dm_o, gb_o, db_o,
    gs_v, ge_v, gm_v, ds_v, de_v, dm_v, stage, q_full, q_dn, sems,
):
    bounds = [first_tile(PER * g) * LANES for g in range(GROUPS + 1)]
    y, core, mine = places()
    for i, block in enumerate((b0, b1, b2, b3, b4, b5, b6, b7)):
        rep = 2 * lax.rem(y - i % 4 + 4, 4) + (core if i < 4 else 1 - core)
        stage[rep] = block[...]

    copies = []

    def send(pairs, at):
        for src, dst in pairs:
            copies.append(pltpu.make_async_copy(src.at[at], dst.at[at], sems.at[len(copies)]))
            copies[-1].start()

    lane = lane_ids()

    def gu_recon(rep, shard):
        return stage[rep, 16 * shard : 16 * shard + 16, :].astype(F32).reshape(2, 8, LANES)

    for g in range(GROUPS):
        for shard in range(PER * g, PER * (g + 1)):
            for j in range(first_tile(shard + 1) - first_tile(shard)):
                recon = gu_recon(j, shard)
                if j == 0 and offset(shard) > 0:
                    other = gu_recon(0 if has_ninth(shard - 1) else 7, shard - 1)
                    recon = jnp.where(lane[None] < offset(shard), other, recon)
                at = (slice(None), slice(None), pl.ds((first_tile(shard) + j) * LANES, LANES))
                gs_v[at] = gs[at] - SLOW_GAIN * recon
                ge_v[at] = (gc[at] - recon).astype(BF16)
                gm_v[at] = gm[at] + recon
        send(
            ((gs_v, gs_o), (ge_v, ge_o), (gm_v, gm_o)),
            (slice(None), slice(None), pl.ds(bounds[g], bounds[g + 1] - bounds[g])),
        )
    tiles = [stage[r, GU_ROWS:BLOCK, :].astype(F32) for r in range(REPS)]
    for shard in range(SHARDS):
        z, x = shard // 4, shard % 4
        q, a = 2 * x + z // 4, z % 4
        for half in range(2):
            recon = None
            for k in range(4):
                piece = tiles[4 * half + k][8 * q : 8 * q + 8]
                if k != a:
                    piece = pltpu.roll(piece, 32 * (k - a) % LANES, 1)
                recon = piece if k == 0 else jnp.where(lane < 32 * k, recon, piece)
            at = (slice(None), pl.ds(DN_COLS * shard + LANES * half, LANES))
            ds_v[at] = ds[at] - SLOW_GAIN * recon
            de_v[at] = (dc[at] - recon).astype(BF16)
            dm_v[at] = dm[at] + recon
    send(((ds_v, ds_o), (de_v, de_o), (dm_v, dm_o)), (slice(None), slice(None)))

    for r in range(REPS):
        block = stage[r, BLOCK:PAYLOAD, :].astype(F32)
        q_full[LANES * r : LANES * r + LANES, :] = block[0:LANES]
        if r == 0:
            q_full[8 * LANES : 9 * LANES, :] = block[0:LANES]
        q_dn[32 * r : 32 * r + 32, :] = block[LANES:Q_ROWS, 0:RANK]
    gb_o[...] = q_full[pl.ds(offset(mine), GU_COLS), :].astype(BF16)
    db_o[...] = q_dn[...].T.astype(BF16)
    for copy in copies:
        copy.wait()


def finish(blocks, parts, dn_parts):
    gu, dn = (2, 8, FF), (8, D)
    kinds = (F32, BF16, F32)
    return pl.pallas_call(
        finish_kernel,
        out_shape=(
            *[jax.ShapeDtypeStruct(gu, kind) for kind in kinds],
            *[jax.ShapeDtypeStruct(dn, kind) for kind in kinds],
            jax.ShapeDtypeStruct((GU_COLS, LANES), BF16),
            jax.ShapeDtypeStruct((RANK, DN_COLS), BF16),
        ),
        in_specs=[VMEM] * 14,
        out_specs=(ANY,) * 6 + (VMEM, VMEM),
        scratch_shapes=[
            *[pltpu.VMEM(gu, kind) for kind in kinds],
            *[pltpu.VMEM(dn, kind) for kind in kinds],
            pltpu.VMEM((REPS, PAYLOAD, LANES), BF16),
            pltpu.VMEM((9 * LANES, LANES), F32),
            pltpu.VMEM((DN_COLS, RANK), F32),
            pltpu.SemaphoreType.DMA((3 * (GROUPS + 1),)),
        ],
        compiler_params=params(32),
    )(*blocks, *parts, *dn_parts)


MOMENT_GAIN = 0.7 * 0.9 * 0.9
SLOW_GAIN = 0.7 * 1.9


def settled(slow, fast, error, moment):
    combined = slow - fast.astype(F32) + error.astype(F32)
    return slow - MOMENT_GAIN * moment, combined, 0.9 * moment


def shift(value, axis, size, by):
    return lax.ppermute(value, axis, [(i, (i + by) % size) for i in range(size)])


def swap(value):
    return lax.ppermute(value, "core", [(0, 1), (1, 0)])


def exchange(value, axis):
    return lax.all_to_all(value, axis, 0, 0, tiled=False)


def on_device(
    gu_slow, gu_fast, gu_error, gu_moment, gu_basis, dn_slow, dn_fast, dn_error, dn_moment, dn_basis
):
    gu_fast, gu_error = gu_fast[0], gu_error[0]
    dn_fast, dn_error = dn_fast[0], dn_error[0]
    tiles = basis_tiles(gu_basis, dn_basis.T)
    basis = exchange(tiles, "z")
    own, oth = lower(gu_slow, gu_fast, gu_error, dn_slow, dn_fast, dn_error)
    came = swap(oth)
    zero, *sends = pair_sums(own, came, tiles)
    comes = {by: shift(sends[by - 1], "y", 4, by) for by in (2, 1, 3)}
    rows = list(y_sum(zero, comes))
    for by in (2, 1, 3):
        rows[by] = shift(rows[by], "x", 4, by)
    rows, parts = p_part(rows, basis)
    parts = exchange(parts, ("y", "core", "x"))
    recv = exchange(p_sum(parts, rows), "z")
    a_blocks, q_block = factor(recv)
    payload = pack(exchange(a_blocks, SHARD), q_block)
    mine = {0: payload}
    for by in (2, 1, 3):
        mine[by] = shift(payload, "y", 4, by)
    blocks = [mine[by] for by in range(4)]
    blocks = blocks + [swap(b) for b in blocks]
    gs, ge, gm, ds, de, dm, gb, db = finish(
        blocks,
        settled(gu_slow, gu_fast, gu_error, gu_moment),
        settled(dn_slow, dn_fast, dn_error, dn_moment),
    )
    return gs, ge[None], gm, gb, ds, de[None], dm, db.T


def solution(mesh):
    fine = Mesh(mesh.devices.reshape(4, 2, 8, 4), ("y", "core", "z", "x"))
    rep = ("y", "core")
    weights, shared = P(None, SHARD, None), P(SHARD, None)
    replica = P(rep, None, SHARD, None)
    dn_replica = P(rep, SHARD, None)
    return jax.shard_map(
        on_device,
        mesh=fine,
        in_specs=(
            weights, replica, replica, weights, shared,
            shared, dn_replica, dn_replica, shared, shared,
        ),
        out_specs=(
            weights, replica, weights, shared,
            shared, dn_replica, shared, shared,
        ),
        check_vma=False,
    )
```
